768 devices in a mesh: ri: 96 (over z, x, core), ao: 8 (over y).
Axes of the slice: x: 4, y: 8, z: 12, core: 2. Of those that a mesh axis runs over, the one named last changes fastest.
Arguments:
- three_center: bfloat16 [1536, 768, 768], P(('ri', 'ao')), may hold values from -24 to 24
- b_pattern: int32 [1536, 6, 6], P(('ri', 'ao')), may hold values 0 or 1
- density: bfloat16 [768, 768], P('ao')
- d_pattern: int32 [6, 6], replicated, may hold values 0 or 1
Outputs:
- exchange: float32 [768, 768], P('ao', 'ri')
The draws below stay inside these ranges and needn't reach their ends.
All inputs are finite; a program needn't handle non-finite values. No bound on the sum of `b_pattern` on one device may be relied on, other than what follows from the above.
Results may differ from the reference program's by a relative error of at most 0.0029.
Values may be sent and summed in bfloat16 or wider, within the bound.
No kernel may reach another device: no remote copies, remote signals or barrier semaphores. Data moves between devices by JAX's collectives and lax.ppermute only.
A program may use at most 32 MiB of HBM per device.

```python
import math
import jax
import jax.numpy as jnp
from jax import lax

BS = 128
A = 768
NB = 6
R = 1536


def draw_density(key, part):
    key = jax.random.fold_in(key, 7)
    values = jax.random.normal(key, (A, A), jnp.float32)
    symmetric = (values + values.T) * (0.5 / math.sqrt(A))
    return symmetric.astype(jnp.bfloat16)


def touch_ends(values, key, smallest, top_value):
    shape = values.shape
    index_at = [jax.random.randint(jax.random.fold_in(key, axis), (), 0, shape[axis]) for axis in range(len(shape))]
    values = values.at[tuple(index_at)].set(smallest)
    longest = shape.index(max(shape))
    index_at[longest] = (index_at[longest] + 1) % shape[longest]
    return values.at[tuple(index_at)].set(top_value)


def strengthened(values, rng, source, target, blocks, factor):
    owner, partner = [(jnp.arange(values.shape[axis_at]) // (values.shape[axis_at] // blocks)).reshape([-1 if axis == axis_at else 1 for axis in range(values.ndim)]) for axis_at in (source, target)]
    chosen = jax.random.permutation(rng, blocks)[partner]
    strong = (owner == chosen) | (owner == (partner + blocks // 2) % blocks)
    return jnp.where(strong, factor * values, values)


def level_of(key, dims, split, smallest, largest):
    def one(dim, shards_of):
        steps = jax.random.uniform(jax.random.fold_in(jax.random.fold_in(key, 6), dim), (shards_of,), jnp.float32, smallest / len(split), largest / len(split))
        return jnp.repeat(jnp.exp(steps), dims[dim] // shards_of).reshape((-1,) + (1,) * (len(dims) - dim - 1))

    factor_of = one(*split[0])
    for cut in split[1:]:
        factor_of = factor_of * one(*cut)
    return factor_of


def bell_draw_with(stream_key, dims, spread, reach, cuts, heavy, dtype=jnp.bfloat16):
    entries = spread * jax.random.normal(stream_key, dims, jnp.float32)
    if cuts:
        entries = entries * level_of(stream_key, dims, cuts, -0.22, 0.18)
    return jnp.clip(strengthened(entries, jax.random.fold_in(stream_key, 3), *heavy), -reach, reach).astype(dtype)


def setup_inputs(seed: int = 0) -> dict:
    splits = jax.random.split(jax.random.key(seed), 5)
    three_center = bell_draw_with(splits[0], (R, A, A), 1.0, 24.0, ((0, 768),), (0, 1, 768, 6.0))
    b_pattern = touch_ends((jax.random.randint(splits[1], (R, NB, NB), 0, 4) < 3).astype(jnp.int32), jax.random.fold_in(splits[1], 1), 0, 1)
    density = draw_density(jax.random.fold_in(splits[4], 71), 0)
    d_pattern = touch_ends((jax.random.randint(splits[3], (NB, NB), 0, 4) < 3).astype(jnp.int32), jax.random.fold_in(splits[3], 1), 0, 1)
    return dict(three_center=three_center, b_pattern=b_pattern, density=density, d_pattern=d_pattern)


def block_mask(values, pattern, block_size):
    lead = values.shape[:-2]
    rows = values.shape[-2] // block_size
    cols = values.shape[-1] // block_size
    shaped = values.reshape(lead + (rows, block_size, cols, block_size))
    keep = pattern.reshape(lead + (rows, 1, cols, 1)) > 0
    return jnp.where(keep, shaped, jnp.zeros_like(shaped)).reshape(values.shape)

def reference(three_center, b_pattern, density, d_pattern):
    masked_b = block_mask(three_center, b_pattern, BS)
    sym_pattern = jnp.maximum(d_pattern, d_pattern.T)
    masked_d = block_mask(density, sym_pattern, BS)

    def add_term(running, slab):
        half = jnp.dot(slab, masked_d, preferred_element_type=jnp.float32).astype(jnp.bfloat16)
        return (running + jnp.dot(half, slab.T, preferred_element_type=jnp.float32), None)
    total, _ = lax.scan(add_term, jnp.zeros((A, A), jnp.float32), masked_b)
    return total * jnp.float32(1.0 / math.sqrt(R * A))
```

```python
import functools
import math

import jax
import jax.numpy as jnp
from jax import lax
from jax.experimental import pallas as pl
from jax.experimental.pallas import tpu as pltpu
from jax.sharding import Mesh, PartitionSpec as P

Z, X, C, Y = 12, 4, 2, 8
A, BS, NB = 768, 128, 6
K = 8
G = 16
GROUPS = A // G
ROWS = A // (Y * C)
HALF = A // 2
PACK = ROWS * Z * G // 128
MAIN = 128 // G
VMEM = pl.BlockSpec(memory_space=pltpu.VMEM)
SMEM = pl.BlockSpec(memory_space=pltpu.SMEM)
ANY = pl.BlockSpec(memory_space=pl.ANY)


def place(z, x):
    return (x // 2) * 24 + (z if x % 2 == 0 else 12 + (z + 4) % 12)


def mask_kernel(pattern, b_ref, out_ref):
    p = pl.program_id(0)
    for rb in range(NB):
        for cb in range(NB):
            keep = pattern[p, rb, cb] > 0
            lanes = slice(cb * BS, (cb + 1) * BS)
            for g in range(rb * 8, rb * 8 + 8):
                block = b_ref[0, g, :, lanes]
                out_ref[0, place(g // X, g % X), :, lanes] = jnp.where(keep, block, jnp.zeros_like(block))


def mask_and_order(three_center, b_pattern):
    count = three_center.shape[0]
    spec = pl.BlockSpec((1, GROUPS, G, A), lambda p: (p, 0, 0, 0))
    return pl.pallas_call(
        mask_kernel,
        grid=(count,),
        in_specs=[SMEM, spec],
        out_specs=spec,
        out_shape=jax.ShapeDtypeStruct((count, GROUPS, G, A), jnp.bfloat16),
        name="mask",
    )(b_pattern, three_center.reshape(count, GROUPS, G, A))


def exchange_kernel(count, core_ref, d_pattern, d_own, d_other, b_own, b_other, out_ref, b, d, rows, acc, sems):
    copies = []
    for p in range(2 * count):
        source = b_own.at[p] if p < count else b_other.at[p - count]
        copy = pltpu.make_async_copy(source, b.at[p], sems.at[p])
        copy.start()
        copies.append(copy)
    core = core_ref[0]
    for h, half_ref in ((core, d_own), (1 - core, d_other)):
        for rb in range(NB):
            for cb in range(NB // 2):
                col = h * (NB // 2) + cb
                keep = jnp.maximum(d_pattern[rb, col], d_pattern[col, rb]) > 0
                block = half_ref[rb * BS : (rb + 1) * BS, cb * BS : (cb + 1) * BS]
                lanes = pl.ds(pl.multiple_of(col * BS, BS), BS)
                d[rb * BS : (rb + 1) * BS, lanes] = jnp.where(keep, block, jnp.zeros_like(block))
    acc[...] = jnp.zeros_like(acc)
    for p in range(2 * count):
        copies[p].wait()

        for t in range(Y * ROWS // G):
            per = ROWS // G
            g = (t // per) * (C * per) + core * per + t % per
            z, x = lax.div(g, X), lax.rem(g, X)
            z_at = jnp.where(lax.rem(x, 2) == 0, z, 12 + lax.rem(z + 4, 12))
            rows[t * G : (t + 1) * G, :] = b[p, lax.div(x, 2) * 24 + z_at]
        half = jnp.dot(rows[...], d[...], preferred_element_type=jnp.float32).astype(jnp.bfloat16)
        full = b[p].reshape(A, A)
        acc[...] += lax.dot_general(
            half, full, (((1,), (1,)), ((), ())), preferred_element_type=jnp.float32
        )
    lane = lax.broadcasted_iota(jnp.int32, (ROWS // 2, 128), 1)
    for y in range(Y):
        for q in range(X // 2):
            block = acc[y * ROWS : (y + 1) * ROWS, q * HALF : (q + 1) * HALF]
            first, middle, last = block[:, :128], block[:, 128:256], block[:, 256:]
            turned = pltpu.roll(middle, 64, 1)
            top, bottom = slice(0, ROWS // 2), slice(ROWS // 2, ROWS)
            even = jnp.where(lane < 64, middle[top], turned[bottom])
            odd = jnp.where(lane < 64, turned[top], middle[bottom])
            out_ref[(2 * q) * Y + y] = jnp.concatenate([first, even], 0).astype(jnp.bfloat16)
            out_ref[(2 * q + 1) * Y + y] = jnp.concatenate([last, odd], 0).astype(jnp.bfloat16)


def exchange_rows(core, d_pattern, d_own, d_other, b_own, b_other):
    count = b_own.shape[0]
    return pl.pallas_call(
        functools.partial(exchange_kernel, count),
        in_specs=[SMEM, SMEM, VMEM, VMEM, ANY, ANY],
        out_specs=VMEM,
        out_shape=jax.ShapeDtypeStruct((X * Y, PACK, 128), jnp.bfloat16),
        scratch_shapes=[
            pltpu.VMEM((2 * count, GROUPS, G, A), jnp.bfloat16),
            pltpu.VMEM((A, A), jnp.bfloat16),
            pltpu.VMEM((Y * ROWS, A), jnp.bfloat16),
            pltpu.VMEM((Y * ROWS, A), jnp.float32),
            pltpu.SemaphoreType.DMA((2 * count,)),
        ],
        compiler_params=pltpu.CompilerParams(vmem_limit_bytes=40 * 1024 * 1024),
        name="exchange",
    )(core, d_pattern, d_own, d_other, b_own, b_other)


def sum_xy_kernel(in_ref, out_ref):
    total = in_ref[0].astype(jnp.float32)
    for i in range(1, X * Y):
        total = total + in_ref[i].astype(jnp.float32)
    first, rest = total[:ROWS], total[ROWS:]
    first = first.T
    rest = rest.T
    rest = jnp.concatenate([rest[:64], rest[64:]], 1)
    for i in range(Z * C):
        part = first[i * K : (i + 1) * K] if i < MAIN * C else rest[i * K - 128 : (i + 1) * K - 128]
        out_ref[i] = part


def sum_xy(parts):
    return pl.pallas_call(
        sum_xy_kernel,
        in_specs=[VMEM],
        out_specs=VMEM,
        out_shape=jax.ShapeDtypeStruct((Z * C, K, ROWS), jnp.float32),
        name="sum_xy",
    )(parts)


def sum_z_kernel(factor, in_ref, out_ref):
    halves = []
    for c in range(C):
        total = in_ref[c]
        for z in range(1, Z):
            total = total + in_ref[z * C + c]
        halves.append(total * factor)
    out_ref[...] = jnp.concatenate(halves, 1)


def sum_z(parts, factor):
    return pl.pallas_call(
        functools.partial(sum_z_kernel, factor),
        in_specs=[VMEM],
        out_specs=VMEM,
        out_shape=jax.ShapeDtypeStruct((K, C * ROWS), jnp.float32),
        name="sum_z",
    )(parts)


def per_device(three_center, b_pattern, density, d_pattern):
    core = lax.axis_index("c")
    swap = [(0, 1), (1, 0)]
    b_own = mask_and_order(three_center, b_pattern)
    b_other = lax.ppermute(b_own, "c", swap)
    mine = lax.dynamic_slice(density, (0, core * HALF), (density.shape[0], HALF))
    mine = jnp.broadcast_to(mine[None], (Y,) + mine.shape)
    d_own = lax.all_to_all(mine, "y", 0, 0, tiled=True).reshape(A, HALF)
    d_other = lax.ppermute(d_own, "c", swap)
    parts = exchange_rows(core.reshape(1), d_pattern, d_own, d_other, b_own, b_other)
    parts = lax.all_to_all(parts, ("x", "y"), 0, 0, tiled=True)
    parts = lax.all_to_all(sum_xy(parts), ("z", "c"), 0, 0, tiled=True)
    total_ri = three_center.shape[0] * Z * X * C * Y
    return sum_z(parts, 1.0 / math.sqrt(total_ri * A)).T


def solution(mesh):
    fine = Mesh(mesh.devices.reshape(Z, X, C, Y), ("z", "x", "c", "y"))
    every = ("z", "x", "c", "y")
    return jax.shard_map(
        per_device,
        mesh=fine,
        in_specs=(P(every, None, None), P(every, None, None), P("y", None), P()),
        out_specs=P("y", ("z", "x", "c")),
        check_vma=False,
    )
```

```python
import functools
import math

import jax
import jax.numpy as jnp
from jax import lax
from jax.experimental import pallas as pl
from jax.experimental.pallas import tpu as pltpu
from jax.sharding import Mesh, PartitionSpec as P

Z, X, C, Y = 12, 4, 2, 8
A, BS, NB = 768, 128, 6
K = 8
G = 16
GROUPS = A // G
ROWS = A // (Y * C)
YROWS = A // Y
STEP = 32
SENT = 4
PACK = ROWS * Z * G // 128
MAIN = 128 // G
VMEM = pl.BlockSpec(memory_space=pltpu.VMEM)
SMEM = pl.BlockSpec(memory_space=pltpu.SMEM)
ANY = pl.BlockSpec(memory_space=pl.ANY)


def place(z, x):
    return (x // 2) * 24 + (z if x % 2 == 0 else 12 + (z + 4) % 12)


def mask_kernel(pattern, b_ref, out_ref):
    p = pl.program_id(0)
    for rb in range(NB):
        for cb in range(NB):
            keep = pattern[rb, p, cb] > 0
            lanes = slice(cb * BS, (cb + 1) * BS)
            for g in range(rb * 8, rb * 8 + 8):
                block = b_ref[0, g, :, lanes]
                out_ref[0, place(g // X, g % X), :, lanes] = jnp.where(keep, block, jnp.zeros_like(block))


def mask_and_order(three_center, b_pattern):
    count = three_center.shape[0]
    spec = pl.BlockSpec((1, GROUPS, G, A), lambda p: (p, 0, 0, 0))
    return pl.pallas_call(
        mask_kernel,
        grid=(count,),
        in_specs=[SMEM, spec],
        out_specs=spec,
        out_shape=pltpu.VMEM((count, GROUPS, G, A), jnp.bfloat16),
        name="mask",
    )(b_pattern.transpose(1, 0, 2), three_center.reshape(count, GROUPS, G, A))


def exchange_kernel(count, core_ref, d_pattern, d_own, d_other, b_own, b_other, out_ref, d, acc):
    core = core_ref[0]
    for h, part in ((core, d_own), (1 - core, d_other)):
        for y in range(Y):
            for t in range(YROWS // STEP):
                rb = (y * YROWS + t * STEP) // BS
                here = slice(y * YROWS + t * STEP, y * YROWS + (t + 1) * STEP)
                for j in range(SENT // C):
                    col = lax.rem(rb + h * (SENT // C) + j, NB)
                    keep = jnp.maximum(d_pattern[rb, col], d_pattern[col, rb]) > 0
                    block = part[y, t * STEP : (t + 1) * STEP, j * BS : (j + 1) * BS]
                    lanes = pl.ds(pl.multiple_of(col * BS, BS), BS)
                    d[here, lanes] = jnp.where(keep, block, jnp.zeros_like(block))
    for rb in range(NB):
        for k in range(SENT, NB):
            cb = (rb + k) % NB
            rows, cols = slice(rb * BS, (rb + 1) * BS), slice(cb * BS, (cb + 1) * BS)
            d[rows, cols] = d[cols, rows].T
    for p in range(2 * count):
        b = b_own.at[p] if p < count else b_other.at[p - count]
        full = b[...].reshape(A, A)
        for q in range(X // 2):
            rows = b[pl.ds(q * 2 * Z + core * Z, Z)].reshape(Z * G, A)
            half = jnp.dot(rows, d[...], preferred_element_type=jnp.float32).astype(jnp.bfloat16)
            term = lax.dot_general(half, full, (((1,), (1,)), ((), ())), preferred_element_type=jnp.float32)
            here = slice(q * Z * G, (q + 1) * Z * G)
            acc[here, :] = term if p == 0 else acc[here, :] + term
    lane = lax.broadcasted_iota(jnp.int32, (ROWS // 2, 128), 1)
    top, bottom = slice(0, ROWS // 2), slice(ROWS // 2, ROWS)
    for y in range(Y):
        groups = []
        for t in range(ROWS // G):
            g = y * (YROWS // G) + 2 * t
            z, q = g // X, (g % X) // 2
            at = q * Z + jnp.where(core == 0, z, (z + Z - MAIN) % Z)
            groups.append(acc[pl.ds(pl.multiple_of(at * G, G), G), :])
        for q in range(X // 2):
            first, middle, last = [
                jnp.concatenate([g[:, (3 * q + i) * 128 : (3 * q + i + 1) * 128] for g in groups], 0)
                for i in range(3)
            ]
            turned = pltpu.roll(middle, 64, 1)
            even = jnp.where(lane < 64, middle[top], turned[bottom])
            odd = jnp.where(lane < 64, turned[top], middle[bottom])
            out_ref[(2 * q) * Y + y] = jnp.concatenate([first, even], 0).astype(jnp.bfloat16)
            out_ref[(2 * q + 1) * Y + y] = jnp.concatenate([last, odd], 0).astype(jnp.bfloat16)


def exchange_rows(core, d_pattern, d_own, d_other, b_own, b_other):
    count = b_own.shape[0]
    return pl.pallas_call(
        functools.partial(exchange_kernel, count),
        in_specs=[SMEM, SMEM, VMEM, VMEM, VMEM, VMEM],
        out_specs=VMEM,
        out_shape=pltpu.VMEM((X * Y, PACK, 128), jnp.bfloat16),
        scratch_shapes=[
            pltpu.VMEM((A, A), jnp.bfloat16),
            pltpu.VMEM((Y * ROWS, A), jnp.float32),
        ],
        compiler_params=pltpu.CompilerParams(vmem_limit_bytes=40 * 1024 * 1024),
        name="exchange",
    )(core, d_pattern, d_own, d_other, b_own, pltpu.with_memory_space_constraint(b_other, pltpu.VMEM))


def pack_kernel(place_ref, density, out_ref):
    y, core = place_ref[0], place_ref[1]
    for t in range(YROWS // STEP):
        rb = lax.div(y * YROWS + t * STEP, BS)
        for j in range(SENT // C):
            col = lax.rem(rb + core * (SENT // C) + j, NB)
            block = density[t * STEP : (t + 1) * STEP, pl.ds(pl.multiple_of(col * BS, BS), BS)]
            for to in range(Y):
                out_ref[to, t * STEP : (t + 1) * STEP, j * BS : (j + 1) * BS] = block


def pack_density(place_at, density):
    return pl.pallas_call(
        pack_kernel,
        in_specs=[SMEM, VMEM],
        out_specs=VMEM,
        out_shape=pltpu.VMEM((Y, YROWS, SENT // C * BS), jnp.bfloat16),
        name="pack",
    )(place_at, density)


def sum_xy_kernel(in_ref, out_ref):
    total = in_ref[0].astype(jnp.float32)
    for i in range(1, X * Y):
        total = total + in_ref[i].astype(jnp.float32)
    first, rest = total[:ROWS], total[ROWS:]
    first = first.T
    rest = rest.T
    rest = jnp.concatenate([rest[:64], rest[64:]], 1)
    both = jnp.concatenate([first, rest], 0)
    both = jnp.concatenate([both, jnp.zeros((Z * G, 128 - ROWS), jnp.float32)], 1)
    out_ref[...] = both.reshape(Z * C, K, 128)


def sum_xy(parts):
    return pl.pallas_call(
        sum_xy_kernel,
        in_specs=[VMEM],
        out_specs=VMEM,
        out_shape=pltpu.VMEM((Z * C, K, 128), jnp.float32),
        name="sum_xy",
    )(pltpu.with_memory_space_constraint(parts, pltpu.VMEM))


def sum_z_kernel(factor, in_ref, out_ref):
    halves = []
    for c in range(C):
        total = in_ref[c]
        for z in range(1, Z):
            total = total + in_ref[z * C + c]
        halves.append(total * factor)
    out_ref[...] = jnp.concatenate([halves[g % C][:, g // C * G : (g // C + 1) * G] for g in range(YROWS // G)], 1)


def sum_z(parts, factor):
    return pl.pallas_call(
        functools.partial(sum_z_kernel, factor),
        in_specs=[VMEM],
        out_specs=VMEM,
        out_shape=jax.ShapeDtypeStruct((K, YROWS), jnp.float32),
        name="sum_z",
    )(pltpu.with_memory_space_constraint(parts, pltpu.VMEM))


def per_device(three_center, b_pattern, density, d_pattern):
    core, y = lax.axis_index("c"), lax.axis_index("y")
    swap = [(0, 1), (1, 0)]
    mine = pack_density(jnp.stack([y, core]), density)
    mine, b_pattern = lax.optimization_barrier((mine, b_pattern))
    b_own = mask_and_order(three_center, b_pattern)
    b_other = lax.ppermute(b_own, "c", swap)
    d_own = lax.all_to_all(mine, "y", 0, 0, tiled=True)
    d_other = lax.ppermute(d_own, "c", swap)
    parts = exchange_rows(core.reshape(1), d_pattern, d_own, d_other, b_own, b_other)
    parts = lax.all_to_all(parts, ("x", "y"), 0, 0, tiled=True)
    parts = lax.all_to_all(sum_xy(parts), ("z", "c"), 0, 0, tiled=True)
    total_ri = three_center.shape[0] * Z * X * C * Y
    return sum_z(parts, 1.0 / math.sqrt(total_ri * A)).T


def solution(mesh):
    fine = Mesh(mesh.devices.reshape(Z, X, C, Y), ("z", "x", "c", "y"))
    every = ("z", "x", "c", "y")
    return jax.shard_map(
        per_device,
        mesh=fine,
        in_specs=(P(every, None, None), P(every, None, None), P("y", None), P()),
        out_specs=P("y", ("z", "x", "c")),
        check_vma=False,
    )
```

```python
import functools
import math

import jax
import jax.numpy as jnp
from jax import lax
from jax.experimental import pallas as pl
from jax.experimental.pallas import tpu as pltpu
from jax.sharding import Mesh, PartitionSpec as P

Z, X, C, Y = 12, 4, 2, 8
A, BS, NB = 768, 128, 6
K = 8
G = 16
GROUPS = A // G
ROWS = A // (Y * C)
YROWS = A // Y
STEP = 32
SENT = 4
PACK = ROWS * Z * G // 128
MAIN = 128 // G
COST = 10**11
MIB = 1024 * 1024
VMEM = pl.BlockSpec(memory_space=pltpu.VMEM)
SMEM = pl.BlockSpec(memory_space=pltpu.SMEM)
ANY = pl.BlockSpec(memory_space=pl.ANY)


def place(z, x):
    return (x // 2) * 24 + (z if x % 2 == 0 else 12 + (z + 4) % 12)


def mask_kernel(count, pattern, b_ref, *out_refs):
    for p in range(count):
        for rb in range(NB):
            for cb in range(NB):
                keep = pattern[rb, p, cb] > 0
                lanes = slice(cb * BS, (cb + 1) * BS)
                for g in range(rb * 8, rb * 8 + 8):
                    block = b_ref[p, g, :, lanes]
                    q, at = divmod(place(g // X, g % X), 2 * Z)
                    out_refs[p * (X // 2) + q][at, :, lanes] = jnp.where(keep, block, jnp.zeros_like(block))


def mask_and_order(three_center, b_pattern):
    count = three_center.shape[0]
    pieces = count * (X // 2)
    return pl.pallas_call(
        functools.partial(mask_kernel, count),
        in_specs=[SMEM, VMEM],
        out_specs=[VMEM] * pieces,
        out_shape=[pltpu.VMEM((2 * Z, G, A), jnp.bfloat16)] * pieces,
        compiler_params=pltpu.CompilerParams(vmem_limit_bytes=16 * MIB),
        name="mask",
    )(b_pattern.transpose(1, 0, 2), three_center.reshape(count, GROUPS, G, A))


def density_kernel(core_ref, d_pattern, d_own, d_other, d):
    core = core_ref[0]
    for h, part in ((core, d_own), (1 - core, d_other)):
        for y in range(Y):
            for t in range(YROWS // STEP):
                rb = (y * YROWS + t * STEP) // BS
                here = slice(y * YROWS + t * STEP, y * YROWS + (t + 1) * STEP)
                for j in range(SENT // C):
                    col = lax.rem(rb + h * (SENT // C) + j, NB)
                    keep = jnp.maximum(d_pattern[rb, col], d_pattern[col, rb]) > 0
                    block = part[y, t * STEP : (t + 1) * STEP, j * BS : (j + 1) * BS]
                    lanes = pl.ds(pl.multiple_of(col * BS, BS), BS)
                    d[here, lanes] = jnp.where(keep, block, jnp.zeros_like(block))
    for rb in range(NB):
        for k in range(SENT, NB):
            cb = (rb + k) % NB
            rows, cols = slice(rb * BS, (rb + 1) * BS), slice(cb * BS, (cb + 1) * BS)
            d[rows, cols] = d[cols, rows].T


def whole_density(core, d_pattern, d_own, d_other):
    return pl.pallas_call(
        density_kernel,
        in_specs=[SMEM, SMEM, VMEM, VMEM],
        out_specs=VMEM,
        out_shape=pltpu.VMEM((A, A), jnp.bfloat16),
        cost_estimate=pl.CostEstimate(flops=COST, bytes_accessed=0, transcendentals=0),
        compiler_params=pltpu.CompilerParams(vmem_limit_bytes=8 * MIB),
        name="density",
    )(core, d_pattern, d_own, d_other)


def exchange_kernel(core_ref, d, *refs):
    *pieces, out_ref, acc = refs
    core = core_ref[0]
    halves = X // 2
    for p in range(len(pieces) // halves):
        for q in range(halves):
            rows = pieces[p * halves + q][pl.ds(core * Z, Z)].reshape(Z * G, A)
            half = jnp.dot(rows, d[...], preferred_element_type=jnp.float32).astype(jnp.bfloat16)
            here = slice(q * Z * G, (q + 1) * Z * G)
            for to in range(halves):
                full = pieces[p * halves + to][...].reshape(2 * Z * G, A)
                term = lax.dot_general(half, full, (((1,), (1,)), ((), ())), preferred_element_type=jnp.float32)
                cols = slice(to * 2 * Z * G, (to + 1) * 2 * Z * G)
                acc[here, cols] = term if p == 0 else acc[here, cols] + term
    lane = lax.broadcasted_iota(jnp.int32, (ROWS // 2, 128), 1)
    top, bottom = slice(0, ROWS // 2), slice(ROWS // 2, ROWS)
    for y in range(Y):
        groups = []
        for t in range(ROWS // G):
            g = y * (YROWS // G) + 2 * t
            z, q = g // X, (g % X) // 2
            at = q * Z + jnp.where(core == 0, z, (z + Z - MAIN) % Z)
            groups.append(acc[pl.ds(pl.multiple_of(at * G, G), G), :])
        for q in range(X // 2):
            first, middle, last = [
                jnp.concatenate([g[:, (3 * q + i) * 128 : (3 * q + i + 1) * 128] for g in groups], 0)
                for i in range(3)
            ]
            turned = pltpu.roll(middle, 64, 1)
            even = jnp.where(lane < 64, middle[top], turned[bottom])
            odd = jnp.where(lane < 64, turned[top], middle[bottom])
            out_ref[(2 * q) * Y + y] = jnp.concatenate([first, even], 0).astype(jnp.bfloat16)
            out_ref[(2 * q + 1) * Y + y] = jnp.concatenate([last, odd], 0).astype(jnp.bfloat16)


def exchange_rows(core, d, pieces):
    pieces = [pltpu.with_memory_space_constraint(piece, pltpu.VMEM) for piece in pieces]
    return pl.pallas_call(
        exchange_kernel,
        in_specs=[SMEM, VMEM] + [VMEM] * len(pieces),
        out_specs=VMEM,
        out_shape=pltpu.VMEM((X * Y, PACK, 128), jnp.bfloat16),
        scratch_shapes=[pltpu.VMEM((Y * ROWS, A), jnp.float32)],
        compiler_params=pltpu.CompilerParams(vmem_limit_bytes=24 * MIB),
        name="exchange",
    )(core, d, *pieces)


def pack_kernel(y_ref, core_ref, density, out_ref):
    y, core = y_ref[0], core_ref[0]
    for t in range(YROWS // STEP):
        rb = lax.div(y * YROWS + t * STEP, BS)
        for j in range(SENT // C):
            col = lax.rem(rb + core * (SENT // C) + j, NB)
            block = density[t * STEP : (t + 1) * STEP, pl.ds(pl.multiple_of(col * BS, BS), BS)]
            for to in range(Y):
                out_ref[to, t * STEP : (t + 1) * STEP, j * BS : (j + 1) * BS] = block


def pack_density(y, core, density):
    return pl.pallas_call(
        pack_kernel,
        in_specs=[SMEM, SMEM, VMEM],
        out_specs=VMEM,
        out_shape=pltpu.VMEM((Y, YROWS, SENT // C * BS), jnp.bfloat16),
        compiler_params=pltpu.CompilerParams(vmem_limit_bytes=8 * MIB),
        name="pack",
    )(y, core, density)


def sum_xy_kernel(in_ref, out_ref):
    total = in_ref[0].astype(jnp.float32)
    for i in range(1, X * Y):
        total = total + in_ref[i].astype(jnp.float32)
    first, rest = total[:ROWS], total[ROWS:]
    first = first.T
    rest = rest.T
    rest = jnp.concatenate([rest[:64], rest[64:]], 1)
    both = jnp.concatenate([first, rest], 0)
    both = both.reshape(Z * C, K, ROWS)
    pad = jnp.zeros((Z * C, K // 2, 128 - 2 * ROWS), jnp.float32)
    out_ref[...] = jnp.concatenate([both[:, : K // 2], both[:, K // 2 :], pad], 2)


def sum_xy(parts):
    return pl.pallas_call(
        sum_xy_kernel,
        in_specs=[VMEM],
        out_specs=VMEM,
        out_shape=pltpu.VMEM((Z * C, K // 2, 128), jnp.float32),
        compiler_params=pltpu.CompilerParams(vmem_limit_bytes=8 * MIB),
        name="sum_xy",
    )(pltpu.with_memory_space_constraint(parts, pltpu.VMEM))


def sum_z_kernel(factor, in_ref, out_ref):
    halves = []
    for c in range(C):
        total = in_ref[c]
        for z in range(1, Z):
            total = total + in_ref[z * C + c]
        total = jnp.concatenate([total[:, :ROWS], total[:, ROWS : 2 * ROWS]], 0)
        halves.append(total * factor)
    out_ref[...] = jnp.concatenate([halves[g % C][:, g // C * G : (g // C + 1) * G] for g in range(YROWS // G)], 1)


def sum_z(parts, factor):
    return pl.pallas_call(
        functools.partial(sum_z_kernel, factor),
        in_specs=[VMEM],
        out_specs=VMEM,
        out_shape=jax.ShapeDtypeStruct((K, YROWS), jnp.float32),
        compiler_params=pltpu.CompilerParams(vmem_limit_bytes=4 * MIB),
        name="sum_z",
    )(pltpu.with_memory_space_constraint(parts, pltpu.VMEM))


def per_device(three_center, b_pattern, density, d_pattern):
    core, y = lax.axis_index("c").reshape(1), lax.axis_index("y").reshape(1)
    swap = [(0, 1), (1, 0)]
    mine = pack_density(y, core, density)
    mine, b_pattern = lax.optimization_barrier((mine, b_pattern))
    b_own = mask_and_order(three_center, b_pattern)
    b_other = [lax.ppermute(piece, "c", swap) for piece in b_own]
    d_own = lax.all_to_all(mine, "y", 0, 0, tiled=True)
    d_own, *b_other = lax.optimization_barrier((d_own, *b_other))
    d_other = lax.ppermute(d_own, "c", swap)
    d = whole_density(core, d_pattern, d_own, d_other)
    parts = exchange_rows(core, d, [*b_own, *b_other])
    parts = lax.all_to_all(parts, ("x", "y"), 0, 0, tiled=True)
    parts = lax.all_to_all(sum_xy(parts), ("z", "c"), 0, 0, tiled=True)
    total_ri = three_center.shape[0] * Z * X * C * Y
    return sum_z(parts, 1.0 / math.sqrt(total_ri * A)).T


def solution(mesh):
    fine = Mesh(mesh.devices.reshape(Z, X, C, Y), ("z", "x", "c", "y"))
    every = ("z", "x", "c", "y")
    return jax.shard_map(
        per_device,
        mesh=fine,
        in_specs=(P(every, None, None), P(every, None, None), P("y", None), P()),
        out_specs=P("y", ("z", "x", "c")),
        check_vma=False,
    )
```

```python
import functools
import math

import jax
import jax.numpy as jnp
from jax import lax
from jax.experimental import pallas as pl
from jax.experimental.pallas import tpu as pltpu
from jax.sharding import Mesh, PartitionSpec as P

Z, X, C, Y = 12, 4, 2, 8
A, BS, NB = 768, 128, 6
K = 8
G = 16
GROUPS = A // G
ROWS = A // (Y * C)
YROWS = A // Y
STEP = 32
SENT = 4
PACK = ROWS * Z * G // 128
MAIN = 128 // G
COST = 10**11
MIB = 1024 * 1024
VMEM = pl.BlockSpec(memory_space=pltpu.VMEM)
SMEM = pl.BlockSpec(memory_space=pltpu.SMEM)
ANY = pl.BlockSpec(memory_space=pl.ANY)


def hbm(x):
    return pltpu.with_memory_space_constraint(x, pltpu.HBM)


def vmem(x):
    return pltpu.with_memory_space_constraint(x, pltpu.VMEM)


def place(z, x):
    return (x // 2) * 24 + (z if x % 2 == 0 else 12 + (z + 4) % 12)


def mask_kernel(pattern, b_ref, out_ref):
    p = pl.program_id(0)
    for rb in range(NB):
        for cb in range(NB):
            keep = pattern[rb, p, cb] > 0
            lanes = slice(cb * BS, (cb + 1) * BS)
            for g in range(rb * 8, rb * 8 + 8):
                block = b_ref[0, g, :, lanes]
                out_ref[0, place(g // X, g % X), :, lanes] = jnp.where(keep, block, jnp.zeros_like(block))


def mask_and_order(three_center, b_pattern):
    count = three_center.shape[0]
    spec = pl.BlockSpec((1, GROUPS, G, A), lambda p: (p, 0, 0, 0))
    return pl.pallas_call(
        mask_kernel,
        grid=(count,),
        in_specs=[SMEM, spec],
        out_specs=spec,
        out_shape=pltpu.VMEM((count, GROUPS, G, A), jnp.bfloat16),
        cost_estimate=pl.CostEstimate(flops=COST, bytes_accessed=0, transcendentals=0),
        compiler_params=pltpu.CompilerParams(vmem_limit_bytes=16 * MIB),
        name="mask",
    )(hbm(b_pattern.transpose(1, 0, 2)), hbm(three_center.reshape(count, GROUPS, G, A)))


def density_mask_kernel(core_ref, d_pattern, part, out_ref):
    core = core_ref[0]
    for y in range(Y):
        for t in range(YROWS // STEP):
            rb = (y * YROWS + t * STEP) // BS
            here = slice(t * STEP, (t + 1) * STEP)
            for j in range(SENT // C):
                col = lax.rem(rb + core * (SENT // C) + j, NB)
                keep = jnp.maximum(d_pattern[rb, col], d_pattern[col, rb]) > 0
                block = part[y, here, j * BS : (j + 1) * BS]
                out_ref[y, here, j * BS : (j + 1) * BS] = jnp.where(keep, block, jnp.zeros_like(block))


def mask_density(core, d_pattern, part):
    return pl.pallas_call(
        density_mask_kernel,
        in_specs=[SMEM, SMEM, VMEM],
        out_specs=VMEM,
        out_shape=pltpu.VMEM(part.shape, jnp.bfloat16),
        cost_estimate=pl.CostEstimate(flops=COST, bytes_accessed=0, transcendentals=0),
        compiler_params=pltpu.CompilerParams(vmem_limit_bytes=8 * MIB),
        name="density_mask",
    )(core, hbm(d_pattern), vmem(part))


def exchange_kernel(count, core_ref, d_own, d_other, b_own, b_there, out_ref, d, acc, b_other, arrived):
    fetch = pltpu.make_async_copy(b_there, b_other, arrived)
    fetch.start()
    core = core_ref[0]
    for h, part in ((core, d_own), (1 - core, d_other)):
        for y in range(Y):
            for t in range(YROWS // STEP):
                rb = (y * YROWS + t * STEP) // BS
                here = slice(y * YROWS + t * STEP, y * YROWS + (t + 1) * STEP)
                for j in range(SENT // C):
                    col = lax.rem(rb + h * (SENT // C) + j, NB)
                    lanes = pl.ds(pl.multiple_of(col * BS, BS), BS)
                    d[here, lanes] = part[y, t * STEP : (t + 1) * STEP, j * BS : (j + 1) * BS]
    for rb in range(NB):
        for k in range(SENT, NB):
            cb = (rb + k) % NB
            rows, cols = slice(rb * BS, (rb + 1) * BS), slice(cb * BS, (cb + 1) * BS)
            d[rows, cols] = d[cols, rows].T
    for p in range(2 * count):
        if p == count:
            fetch.wait()
        b = b_own.at[p] if p < count else b_other.at[p - count]
        full = b[...].reshape(A, A)
        for q in range(X // 2):
            rows = b[pl.ds(q * 2 * Z + core * Z, Z)].reshape(Z * G, A)
            half = jnp.dot(rows, d[...], preferred_element_type=jnp.float32).astype(jnp.bfloat16)
            term = lax.dot_general(half, full, (((1,), (1,)), ((), ())), preferred_element_type=jnp.float32)
            here = slice(q * Z * G, (q + 1) * Z * G)
            acc[here, :] = term if p == 0 else acc[here, :] + term
    lane = lax.broadcasted_iota(jnp.int32, (ROWS // 2, 128), 1)
    top, bottom = slice(0, ROWS // 2), slice(ROWS // 2, ROWS)
    for y in range(Y):
        groups = []
        for t in range(ROWS // G):
            g = y * (YROWS // G) + 2 * t
            z, q = g // X, (g % X) // 2
            at = q * Z + jnp.where(core == 0, z, (z + Z - MAIN) % Z)
            groups.append(acc[pl.ds(pl.multiple_of(at * G, G), G), :])
        for q in range(X // 2):
            first, middle, last = [
                jnp.concatenate([g[:, (3 * q + i) * 128 : (3 * q + i + 1) * 128] for g in groups], 0)
                for i in range(3)
            ]
            turned = pltpu.roll(middle, 64, 1)
            even = jnp.where(lane < 64, middle[top], turned[bottom])
            odd = jnp.where(lane < 64, turned[top], middle[bottom])
            out_ref[(2 * q) * Y + y] = jnp.concatenate([first, even], 0).astype(jnp.bfloat16)
            out_ref[(2 * q + 1) * Y + y] = jnp.concatenate([last, odd], 0).astype(jnp.bfloat16)


def exchange_rows(core, d_own, d_other, b_own, b_other):
    count = b_own.shape[0]
    return pl.pallas_call(
        functools.partial(exchange_kernel, count),
        in_specs=[SMEM, VMEM, VMEM, VMEM, ANY],
        out_specs=VMEM,
        out_shape=pltpu.VMEM((X * Y, PACK, 128), jnp.bfloat16),
        scratch_shapes=[
            pltpu.VMEM((A, A), jnp.bfloat16),
            pltpu.VMEM((Y * ROWS, A), jnp.float32),
            pltpu.VMEM(b_other.shape, jnp.bfloat16),
            pltpu.SemaphoreType.DMA,
        ],
        compiler_params=pltpu.CompilerParams(vmem_limit_bytes=24 * MIB),
        name="exchange",
    )(core, vmem(d_own), vmem(d_other), vmem(b_own), b_other)


def pack_kernel(y_ref, core_ref, density, out_ref):
    y, core = y_ref[0], core_ref[0]
    for t in range(YROWS // STEP):
        rb = lax.div(y * YROWS + t * STEP, BS)
        for j in range(SENT // C):
            col = lax.rem(rb + core * (SENT // C) + j, NB)
            block = density[t * STEP : (t + 1) * STEP, pl.ds(pl.multiple_of(col * BS, BS), BS)]
            for to in range(Y):
                out_ref[to, t * STEP : (t + 1) * STEP, j * BS : (j + 1) * BS] = block


def pack_density(y, core, density):
    return pl.pallas_call(
        pack_kernel,
        in_specs=[SMEM, SMEM, VMEM],
        out_specs=VMEM,
        out_shape=pltpu.VMEM((Y, YROWS, SENT // C * BS), jnp.bfloat16),
        compiler_params=pltpu.CompilerParams(vmem_limit_bytes=8 * MIB),
        name="pack",
    )(y, core, hbm(density))


def sum_xy_kernel(in_ref, out_ref):
    total = in_ref[0].astype(jnp.float32)
    for i in range(1, X * Y):
        total = total + in_ref[i].astype(jnp.float32)
    first, rest = total[:ROWS], total[ROWS:]
    first = first.T
    rest = rest.T
    rest = jnp.concatenate([rest[:64], rest[64:]], 1)
    both = jnp.concatenate([first, rest], 0)
    both = both.reshape(Z * C, K, ROWS)
    pad = jnp.zeros((Z * C, K // 2, 128 - 2 * ROWS), jnp.float32)
    out_ref[...] = jnp.concatenate([both[:, : K // 2], both[:, K // 2 :], pad], 2)


def sum_xy(parts):
    return pl.pallas_call(
        sum_xy_kernel,
        in_specs=[VMEM],
        out_specs=VMEM,
        out_shape=pltpu.VMEM((Z * C, K // 2, 128), jnp.float32),
        compiler_params=pltpu.CompilerParams(vmem_limit_bytes=8 * MIB),
        name="sum_xy",
    )(vmem(parts))


def sum_z_kernel(factor, in_ref, out_ref):
    halves = []
    for c in range(C):
        total = in_ref[c]
        for z in range(1, Z):
            total = total + in_ref[z * C + c]
        total = jnp.concatenate([total[:, :ROWS], total[:, ROWS : 2 * ROWS]], 0)
        halves.append(total * factor)
    out_ref[...] = jnp.concatenate([halves[g % C][:, g // C * G : (g // C + 1) * G] for g in range(YROWS // G)], 1)


def sum_z(parts, factor):
    return pl.pallas_call(
        functools.partial(sum_z_kernel, factor),
        in_specs=[VMEM],
        out_specs=VMEM,
        out_shape=jax.ShapeDtypeStruct((K, YROWS), jnp.float32),
        compiler_params=pltpu.CompilerParams(vmem_limit_bytes=4 * MIB),
        name="sum_z",
    )(vmem(parts))


def per_device(three_center, b_pattern, density, d_pattern):
    core, y = lax.axis_index("c").reshape(1), lax.axis_index("y").reshape(1)
    swap = [(0, 1), (1, 0)]
    mine = pack_density(y, core, density)
    mine, b_pattern = lax.optimization_barrier((mine, b_pattern))
    b_own = mask_and_order(three_center, b_pattern)
    b_other = lax.ppermute(b_own, "c", swap)
    d_own = mask_density(core, d_pattern, lax.all_to_all(mine, "y", 0, 0, tiled=True))
    d_own, b_other = lax.optimization_barrier((d_own, b_other))
    d_other = lax.ppermute(d_own, "c", swap)
    parts = exchange_rows(core, d_own, d_other, b_own, b_other)
    parts = lax.all_to_all(parts, ("x", "y"), 0, 0, tiled=True)
    parts = lax.all_to_all(sum_xy(parts), ("z", "c"), 0, 0, tiled=True)
    total_ri = three_center.shape[0] * Z * X * C * Y
    return sum_z(parts, 1.0 / math.sqrt(total_ri * A)).T


def solution(mesh):
    fine = Mesh(mesh.devices.reshape(Z, X, C, Y), ("z", "x", "c", "y"))
    every = ("z", "x", "c", "y")
    return jax.shard_map(
        per_device,
        mesh=fine,
        in_specs=(P(every, None, None), P(every, None, None), P("y", None), P()),
        out_specs=P("y", ("z", "x", "c")),
        check_vma=False,
    )
```

```python
import functools
import math

import jax
import jax.numpy as jnp
from jax import lax
from jax.experimental import pallas as pl
from jax.experimental.pallas import tpu as pltpu
from jax.sharding import Mesh, PartitionSpec as P

Z, X, C, Y = 12, 4, 2, 8
A, BS, NB = 768, 128, 6
K = 8
G = 16
GROUPS = A // G
ROWS = A // (Y * C)
YROWS = A // Y
STEP = 32
SENT = 4
PACK = ROWS * Z * G // 128
MAIN = 128 // G
COST = 10**11
MIB = 1024 * 1024
VMEM = pl.BlockSpec(memory_space=pltpu.VMEM)
SMEM = pl.BlockSpec(memory_space=pltpu.SMEM)
ANY = pl.BlockSpec(memory_space=pl.ANY)


def hbm(x):
    return pltpu.with_memory_space_constraint(x, pltpu.HBM)


def vmem(x):
    return pltpu.with_memory_space_constraint(x, pltpu.VMEM)


def place(z, x):
    return x * Z + z


def mask_kernel(pattern, b_ref, out_ref):
    p = pl.program_id(0)
    for rb in range(NB):
        for cb in range(NB):
            keep = pattern[rb, p, cb] > 0
            lanes = slice(cb * BS, (cb + 1) * BS)
            for g in range(rb * 8, rb * 8 + 8):
                block = b_ref[0, g, :, lanes]
                out_ref[0, place(g // X, g % X), :, lanes] = jnp.where(keep, block, jnp.zeros_like(block))


def mask_and_order(three_center, b_pattern):
    count = three_center.shape[0]
    spec = pl.BlockSpec((1, GROUPS, G, A), lambda p: (p, 0, 0, 0))
    return pl.pallas_call(
        mask_kernel,
        grid=(count,),
        in_specs=[SMEM, spec],
        out_specs=spec,
        out_shape=pltpu.VMEM((count, GROUPS, G, A), jnp.bfloat16),
        cost_estimate=pl.CostEstimate(flops=COST, bytes_accessed=0, transcendentals=0),
        compiler_params=pltpu.CompilerParams(vmem_limit_bytes=16 * MIB),
        name="mask",
    )(hbm(b_pattern.transpose(1, 0, 2)), hbm(three_center.reshape(count, GROUPS, G, A)))


def settle(part):
    return pl.pallas_call(
        lambda in_ref, out_ref: None,
        in_specs=[ANY],
        out_specs=ANY,
        out_shape=jax.ShapeDtypeStruct(part.shape, part.dtype),
        input_output_aliases={0: 0},
        cost_estimate=pl.CostEstimate(flops=COST, bytes_accessed=0, transcendentals=0),
        compiler_params=pltpu.CompilerParams(vmem_limit_bytes=MIB),
        name="settle",
    )(part)


def exchange_kernel(count, d_own, d_other, b_own, b_there, out_ref, d, acc, b_other, arrived):
    fetch = pltpu.make_async_copy(b_there, b_other, arrived)
    fetch.start()
    core = lax.axis_index("c")
    for h, part in ((core, d_own), (1 - core, d_other)):
        for y in range(Y):
            for t in range(YROWS // STEP):
                rb = (y * YROWS + t * STEP) // BS
                here = slice(y * YROWS + t * STEP, y * YROWS + (t + 1) * STEP)
                for j in range(SENT // C):
                    col = lax.rem(rb + h * (SENT // C) + j, NB)
                    lanes = pl.ds(pl.multiple_of(col * BS, BS), BS)
                    d[here, lanes] = part[y, t * STEP : (t + 1) * STEP, j * BS : (j + 1) * BS]
    for rb in range(NB):
        for k in range(SENT, NB):
            cb = (rb + k) % NB
            rows, cols = slice(rb * BS, (rb + 1) * BS), slice(cb * BS, (cb + 1) * BS)
            d[rows, cols] = d[cols, rows].T
    lane = lax.broadcasted_iota(jnp.int32, (ROWS // 2, 128), 1)
    top, bottom = slice(0, ROWS // 2), slice(ROWS // 2, ROWS)
    half_rows, halves = Z * G, X // 2
    for p in range(2 * count):
        if p == count:
            fetch.wait()
        b = b_own.at[p] if p < count else b_other.at[p - count]
        rows = [b[pl.ds((2 * q + core) * Z, Z)].reshape(half_rows, A) for q in range(halves)]
        half = jnp.dot(jnp.concatenate(rows, 0), d[...], preferred_element_type=jnp.float32).astype(jnp.bfloat16)
        for q in range(halves):
            full = b[q * 2 * Z : (q + 1) * 2 * Z].reshape(2 * half_rows, A)
            term = lax.dot_general(half, full, (((1,), (1,)), ((), ())), preferred_element_type=jnp.float32)
            cols = slice(q * 2 * half_rows, (q + 1) * 2 * half_rows)
            total = term if p == 0 else acc[:, cols] + term
            if p < 2 * count - 1:
                acc[:, cols] = total
                continue
            for y in range(Y):
                groups = []
                for t in range(ROWS // G):
                    z, x = divmod(y * (YROWS // G) + 2 * t, X)
                    at = (x // 2) * half_rows + z * G
                    groups.append(total[at : at + G])
                block = jnp.concatenate(groups, 0)
                first, middle, last = block[:, :128], block[:, 128:256], block[:, 256:]
                turned = pltpu.roll(middle, 64, 1)
                even = jnp.where(lane < 64, middle[top], turned[bottom])
                odd = jnp.where(lane < 64, turned[top], middle[bottom])
                out_ref[(2 * q) * Y + y] = jnp.concatenate([first, even], 0).astype(jnp.bfloat16)
                out_ref[(2 * q + 1) * Y + y] = jnp.concatenate([last, odd], 0).astype(jnp.bfloat16)


def exchange_rows(d_own, d_other, b_own, b_other):
    count = b_own.shape[0]
    return pl.pallas_call(
        functools.partial(exchange_kernel, count),
        in_specs=[VMEM, VMEM, VMEM, ANY],
        out_specs=VMEM,
        out_shape=pltpu.VMEM((X * Y, PACK, 128), jnp.bfloat16),
        scratch_shapes=[
            pltpu.VMEM((A, A), jnp.bfloat16),
            pltpu.VMEM((Y * ROWS, A), jnp.float32),
            pltpu.VMEM(b_other.shape, jnp.bfloat16),
            pltpu.SemaphoreType.DMA,
        ],
        compiler_params=pltpu.CompilerParams(vmem_limit_bytes=24 * MIB),
        name="exchange",
    )(vmem(d_own), vmem(d_other), vmem(b_own), b_other)


def pack_kernel(d_pattern, density, out_ref):
    y, core = lax.axis_index("y"), lax.axis_index("c")
    for t in range(YROWS // STEP):
        rb = lax.div(y * YROWS + t * STEP, BS)
        for j in range(SENT // C):
            col = lax.rem(rb + core * (SENT // C) + j, NB)
            keep = jnp.maximum(d_pattern[rb, col], d_pattern[col, rb]) > 0
            block = density[t * STEP : (t + 1) * STEP, pl.ds(pl.multiple_of(col * BS, BS), BS)]
            block = jnp.where(keep, block, jnp.zeros_like(block))
            for to in range(Y):
                out_ref[to, t * STEP : (t + 1) * STEP, j * BS : (j + 1) * BS] = block


def pack_density(d_pattern, density):
    return pl.pallas_call(
        pack_kernel,
        in_specs=[SMEM, VMEM],
        out_specs=VMEM,
        out_shape=pltpu.VMEM((Y, YROWS, SENT // C * BS), jnp.bfloat16),
        compiler_params=pltpu.CompilerParams(vmem_limit_bytes=8 * MIB),
        name="pack",
    )(hbm(d_pattern), hbm(density))


def sum_xy_kernel(in_ref, out_ref):
    total = in_ref[0].astype(jnp.float32)
    for i in range(1, X * Y):
        total = total + in_ref[i].astype(jnp.float32)
    first, rest = total[:ROWS].T, total[ROWS:].T
    rest = jnp.concatenate([rest[:64], rest[64:]], 1)
    odd = lax.rem(lax.axis_index("x"), 2)
    for part, at in ((first, odd * (Z - MAIN) * C), (rest, (1 - odd) * MAIN * C)):
        count = part.shape[0] // K
        part = part.reshape(count, K, ROWS)
        pad = jnp.zeros((count, K // 2, 128 - 2 * ROWS), jnp.float32)
        out_ref[pl.ds(at, count)] = jnp.concatenate([part[:, : K // 2], part[:, K // 2 :], pad], 2)


def sum_xy(parts):
    return pl.pallas_call(
        sum_xy_kernel,
        in_specs=[VMEM],
        out_specs=VMEM,
        out_shape=pltpu.VMEM((Z * C, K // 2, 128), jnp.float32),
        compiler_params=pltpu.CompilerParams(vmem_limit_bytes=8 * MIB),
        name="sum_xy",
    )(vmem(parts))


def sum_z_kernel(factor, in_ref, out_ref):
    halves = []
    for c in range(C):
        total = in_ref[c]
        for z in range(1, Z):
            total = total + in_ref[z * C + c]
        total = jnp.concatenate([total[:, :ROWS], total[:, ROWS : 2 * ROWS]], 0)
        halves.append(total * factor)
    out_ref[...] = jnp.concatenate([halves[g % C][:, g // C * G : (g // C + 1) * G] for g in range(YROWS // G)], 1)


def sum_z(parts, factor):
    return pl.pallas_call(
        functools.partial(sum_z_kernel, factor),
        in_specs=[VMEM],
        out_specs=VMEM,
        out_shape=jax.ShapeDtypeStruct((K, YROWS), jnp.float32),
        compiler_params=pltpu.CompilerParams(vmem_limit_bytes=4 * MIB),
        name="sum_z",
    )(vmem(parts))


def per_device(three_center, b_pattern, density, d_pattern):
    swap = [(0, 1), (1, 0)]
    mine = pack_density(d_pattern, density)
    mine, b_pattern = lax.optimization_barrier((mine, b_pattern))
    b_own = mask_and_order(three_center, b_pattern)
    b_other = lax.ppermute(b_own, "c", swap)
    d_own = settle(lax.all_to_all(mine, "y", 0, 0, tiled=True))
    d_own, b_other = lax.optimization_barrier((d_own, b_other))
    d_other = lax.ppermute(d_own, "c", swap)
    parts = exchange_rows(d_own, d_other, b_own, b_other)
    parts = lax.all_to_all(parts, ("x", "y"), 0, 0, tiled=True)
    parts = lax.all_to_all(sum_xy(parts), ("z", "c"), 0, 0, tiled=True)
    total_ri = three_center.shape[0] * Z * X * C * Y
    return sum_z(parts, 1.0 / math.sqrt(total_ri * A)).T


def solution(mesh):
    fine = Mesh(mesh.devices.reshape(Z, X, C, Y), ("z", "x", "c", "y"))
    every = ("z", "x", "c", "y")
    return jax.shard_map(
        per_device,
        mesh=fine,
        in_specs=(P(every, None, None), P(every, None, None), P("y", None), P()),
        out_specs=P("y", ("z", "x", "c")),
        check_vma=False,
    )
```

```python
import functools
import math

import jax
import jax.numpy as jnp
from jax import lax
from jax.experimental import pallas as pl
from jax.experimental.pallas import tpu as pltpu
from jax.sharding import Mesh, PartitionSpec as P

Z, X, C, Y = 12, 4, 2, 8
A, BS, NB = 768, 128, 6
K = 8
G = 16
GROUPS = A // G
ROWS = A // (Y * C)
YROWS = A // Y
STEP = 32
SENT = 4
PACK = ROWS * Z * G // 128
MAIN = 128 // G
COST = 10**11
MIB = 1024 * 1024
VMEM = pl.BlockSpec(memory_space=pltpu.VMEM)
SMEM = pl.BlockSpec(memory_space=pltpu.SMEM)
ANY = pl.BlockSpec(memory_space=pl.ANY)


def hbm(x):
    return pltpu.with_memory_space_constraint(x, pltpu.HBM)


def vmem(x):
    return pltpu.with_memory_space_constraint(x, pltpu.VMEM)


def place(z, x):
    return x * Z + z


def mask_kernel(pattern, b_ref, out_ref):
    p = pl.program_id(0)
    for rb in range(NB):
        for cb in range(NB):
            keep = pattern[rb, p, cb] > 0
            lanes = slice(cb * BS, (cb + 1) * BS)
            for g in range(rb * 8, rb * 8 + 8):
                block = b_ref[0, g, :, lanes]
                out_ref[0, place(g // X, g % X), :, lanes] = jnp.where(keep, block, jnp.zeros_like(block))


def mask_and_order(three_center, b_pattern):
    count = three_center.shape[0]
    spec = pl.BlockSpec((1, GROUPS, G, A), lambda p: (p, 0, 0, 0))
    return pl.pallas_call(
        mask_kernel,
        grid=(count,),
        in_specs=[SMEM, spec],
        out_specs=spec,
        out_shape=pltpu.VMEM((count, GROUPS, G, A), jnp.bfloat16),
        cost_estimate=pl.CostEstimate(flops=COST, bytes_accessed=0, transcendentals=0),
        compiler_params=pltpu.CompilerParams(vmem_limit_bytes=16 * MIB),
        name="mask",
    )(hbm(b_pattern.transpose(1, 0, 2)), hbm(three_center.reshape(count, GROUPS, G, A)))


def settle(part):
    return pl.pallas_call(
        lambda in_ref, out_ref: None,
        in_specs=[ANY],
        out_specs=ANY,
        out_shape=jax.ShapeDtypeStruct(part.shape, part.dtype),
        input_output_aliases={0: 0},
        cost_estimate=pl.CostEstimate(flops=COST, bytes_accessed=0, transcendentals=0),
        compiler_params=pltpu.CompilerParams(vmem_limit_bytes=MIB),
        name="settle",
    )(part)


def bring_kernel(*refs):
    arrived = refs[-1]
    count = len(refs) // 2
    copies = [pltpu.make_async_copy(refs[i], refs[count + i], arrived.at[i]) for i in range(count)]
    for copy in copies:
        copy.start()
    for copy in copies:
        copy.wait()


def bring(*there):
    return pl.pallas_call(
        bring_kernel,
        in_specs=[ANY] * len(there),
        out_specs=[VMEM] * len(there),
        out_shape=[pltpu.VMEM(x.shape, x.dtype) for x in there],
        scratch_shapes=[pltpu.SemaphoreType.DMA((len(there),))],
        cost_estimate=pl.CostEstimate(flops=0, bytes_accessed=sum(x.size * 4 for x in there), transcendentals=0),
        compiler_params=pltpu.CompilerParams(vmem_limit_bytes=MIB),
        name="bring",
    )(*there)


def exchange_kernel(count, d_own, d_other, b_own, b_other, out_ref, d, acc):
    core = lax.axis_index("c")
    for h, part in ((core, d_own), (1 - core, d_other)):
        for y in range(Y):
            for t in range(YROWS // STEP):
                rb = (y * YROWS + t * STEP) // BS
                here = slice(y * YROWS + t * STEP, y * YROWS + (t + 1) * STEP)
                for j in range(SENT // C):
                    col = lax.rem(rb + h * (SENT // C) + j, NB)
                    lanes = pl.ds(pl.multiple_of(col * BS, BS), BS)
                    d[here, lanes] = part[y, t * STEP : (t + 1) * STEP, j * BS : (j + 1) * BS]
    for rb in range(NB):
        for k in range(SENT, NB):
            cb = (rb + k) % NB
            rows, cols = slice(rb * BS, (rb + 1) * BS), slice(cb * BS, (cb + 1) * BS)
            d[rows, cols] = d[cols, rows].T
    lane = lax.broadcasted_iota(jnp.int32, (ROWS // 2, 128), 1)
    top, bottom = slice(0, ROWS // 2), slice(ROWS // 2, ROWS)
    half_rows, halves = Z * G, X // 2
    for p in range(2 * count):
        b = b_own.at[p] if p < count else b_other.at[p - count]
        full = b[...].reshape(A, A)
        rows = [b[pl.ds((2 * q + core) * Z, Z)].reshape(half_rows, A) for q in range(halves)]
        half = jnp.dot(jnp.concatenate(rows, 0), d[...], preferred_element_type=jnp.float32).astype(jnp.bfloat16)
        term = lax.dot_general(half, full, (((1,), (1,)), ((), ())), preferred_element_type=jnp.float32)
        acc[...] = term if p == 0 else acc[...] + term
    for y in range(Y):
        at = []
        for t in range(ROWS // G):
            z, x = divmod(y * (YROWS // G) + 2 * t, X)
            at.append((x // 2) * half_rows + z * G)
        for q in range(halves):
            left, middle, right = [
                jnp.concatenate([acc[r : r + G, (3 * q + i) * 128 : (3 * q + i + 1) * 128] for r in at], 0)
                for i in range(3)
            ]
            turned = pltpu.roll(middle, 64, 1)
            even = jnp.where(lane < 64, middle[top], turned[bottom])
            odd = jnp.where(lane < 64, turned[top], middle[bottom])
            out_ref[(2 * q) * Y + y] = jnp.concatenate([left, even], 0).astype(jnp.bfloat16)
            out_ref[(2 * q + 1) * Y + y] = jnp.concatenate([right, odd], 0).astype(jnp.bfloat16)


def exchange_rows(d_own, d_other, b_own, b_other):
    count = b_own.shape[0]
    return pl.pallas_call(
        functools.partial(exchange_kernel, count),
        in_specs=[VMEM, VMEM, VMEM, VMEM],
        out_specs=VMEM,
        out_shape=pltpu.VMEM((X * Y, PACK, 128), jnp.bfloat16),
        scratch_shapes=[
            pltpu.VMEM((A, A), jnp.bfloat16),
            pltpu.VMEM((Y * ROWS, A), jnp.float32),
        ],
        compiler_params=pltpu.CompilerParams(vmem_limit_bytes=24 * MIB),
        name="exchange",
    )(vmem(d_own), vmem(d_other), vmem(b_own), vmem(b_other))


def pack_kernel(d_pattern, density, out_ref):
    y, core = lax.axis_index("y"), lax.axis_index("c")
    for t in range(YROWS // STEP):
        rb = lax.div(y * YROWS + t * STEP, BS)
        for j in range(SENT // C):
            col = lax.rem(rb + core * (SENT // C) + j, NB)
            keep = jnp.maximum(d_pattern[rb, col], d_pattern[col, rb]) > 0
            block = density[t * STEP : (t + 1) * STEP, pl.ds(pl.multiple_of(col * BS, BS), BS)]
            block = jnp.where(keep, block, jnp.zeros_like(block))
            for to in range(Y):
                out_ref[to, t * STEP : (t + 1) * STEP, j * BS : (j + 1) * BS] = block


def pack_density(d_pattern, density):
    return pl.pallas_call(
        pack_kernel,
        in_specs=[SMEM, VMEM],
        out_specs=VMEM,
        out_shape=pltpu.VMEM((Y, YROWS, SENT // C * BS), jnp.bfloat16),
        compiler_params=pltpu.CompilerParams(vmem_limit_bytes=8 * MIB),
        name="pack",
    )(hbm(d_pattern), hbm(density))


def sum_xy_kernel(in_ref, out_ref):
    total = in_ref[0].astype(jnp.float32)
    for i in range(1, X * Y):
        total = total + in_ref[i].astype(jnp.float32)
    first, rest = total[:ROWS].T, total[ROWS:].T
    rest = jnp.concatenate([rest[:64], rest[64:]], 1)
    odd = lax.rem(lax.axis_index("x"), 2)
    for part, at in ((first, odd * (Z - MAIN) * C), (rest, (1 - odd) * MAIN * C)):
        count = part.shape[0] // K
        part = part.reshape(count, K, ROWS)
        pad = jnp.zeros((count, K // 2, 128 - 2 * ROWS), jnp.float32)
        out_ref[pl.ds(at, count)] = jnp.concatenate([part[:, : K // 2], part[:, K // 2 :], pad], 2)


def sum_xy(parts):
    return pl.pallas_call(
        sum_xy_kernel,
        in_specs=[VMEM],
        out_specs=VMEM,
        out_shape=pltpu.VMEM((Z * C, K // 2, 128), jnp.float32),
        compiler_params=pltpu.CompilerParams(vmem_limit_bytes=8 * MIB),
        name="sum_xy",
    )(vmem(parts))


def sum_z_kernel(factor, in_ref, out_ref):
    halves = []
    for c in range(C):
        total = in_ref[c]
        for z in range(1, Z):
            total = total + in_ref[z * C + c]
        total = jnp.concatenate([total[:, :ROWS], total[:, ROWS : 2 * ROWS]], 0)
        halves.append(total * factor)
    out_ref[...] = jnp.concatenate([halves[g % C][:, g // C * G : (g // C + 1) * G] for g in range(YROWS // G)], 1)


def sum_z(parts, factor):
    return pl.pallas_call(
        functools.partial(sum_z_kernel, factor),
        in_specs=[VMEM],
        out_specs=VMEM,
        out_shape=jax.ShapeDtypeStruct((K, YROWS), jnp.float32),
        compiler_params=pltpu.CompilerParams(vmem_limit_bytes=4 * MIB),
        name="sum_z",
    )(vmem(parts))


def per_device(three_center, b_pattern, density, d_pattern):
    swap = [(0, 1), (1, 0)]
    mine = pack_density(d_pattern, density)
    mine, b_pattern = lax.optimization_barrier((mine, b_pattern))
    b_own = mask_and_order(three_center, b_pattern)
    b_other = lax.ppermute(b_own, "c", swap)
    d_own = settle(lax.all_to_all(mine, "y", 0, 0, tiled=True))
    d_own, b_own, b_other = lax.optimization_barrier((d_own, b_own, b_other))
    d_other = lax.ppermute(d_own, "c", swap)
    parts = exchange_rows(d_own, d_other, *bring(b_own, b_other))
    parts = lax.all_to_all(parts, ("x", "y"), 0, 0, tiled=True)
    parts = lax.all_to_all(sum_xy(parts), ("z", "c"), 0, 0, tiled=True)
    total_ri = three_center.shape[0] * Z * X * C * Y
    return sum_z(parts, 1.0 / math.sqrt(total_ri * A)).T


def solution(mesh):
    fine = Mesh(mesh.devices.reshape(Z, X, C, Y), ("z", "x", "c", "y"))
    every = ("z", "x", "c", "y")
    return jax.shard_map(
        per_device,
        mesh=fine,
        in_specs=(P(every, None, None), P(every, None, None), P("y", None), P()),
        out_specs=P("y", ("z", "x", "c")),
        check_vma=False,
    )
```

```python
import functools
import math

import jax
import jax.numpy as jnp
from jax import lax
from jax.experimental import pallas as pl
from jax.experimental.pallas import tpu as pltpu
from jax.sharding import Mesh, PartitionSpec as P

Z, X, C, Y = 12, 4, 2, 8
ZP, YP = Z // 2, Y // 2
A, BS, NB = 768, 128, 6
K = 8
G = 16
GROUPS = A // G
ROWS = A // (Y * C)
YROWS = A // Y
STEP = 32
SENT = 4
UNIT = 2 * G
UNITS = 128 // UNIT
TILES = ZP // 2
COST = 10**11
MIB = 1024 * 1024
VMEM = pl.BlockSpec(memory_space=pltpu.VMEM)
SMEM = pl.BlockSpec(memory_space=pltpu.SMEM)
ANY = pl.BlockSpec(memory_space=pl.ANY)


def hbm(x):
    return pltpu.with_memory_space_constraint(x, pltpu.HBM)


def vmem(x):
    return pltpu.with_memory_space_constraint(x, pltpu.VMEM)


def place(z, x):
    pair, lower = divmod(z, 2)
    return ((x // 2 * TILES + pair // 2) * UNITS + x % 2 * 2 + lower) * 2 + pair % 2


def mask_kernel(pattern, b_ref, out_ref):
    p = pl.program_id(0)
    for rb in range(NB):
        for cb in range(NB):
            keep = pattern[rb, p, cb] > 0
            lanes = slice(cb * BS, (cb + 1) * BS)
            for g in range(rb * 8, rb * 8 + 8):
                block = b_ref[0, g, :, lanes]
                out_ref[0, place(g // X, g % X), :, lanes] = jnp.where(keep, block, jnp.zeros_like(block))


def mask_and_order(three_center, b_pattern):
    count = three_center.shape[0]
    spec = pl.BlockSpec((1, GROUPS, G, A), lambda p: (p, 0, 0, 0))
    return pl.pallas_call(
        mask_kernel,
        grid=(count,),
        in_specs=[SMEM, spec],
        out_specs=spec,
        out_shape=pltpu.VMEM((count, GROUPS, G, A), jnp.bfloat16),
        cost_estimate=pl.CostEstimate(flops=COST, bytes_accessed=0, transcendentals=0),
        compiler_params=pltpu.CompilerParams(vmem_limit_bytes=16 * MIB),
        name="mask",
    )(hbm(b_pattern.transpose(1, 0, 2)), hbm(three_center.reshape(count, GROUPS, G, A)))


def settle(part):
    return pl.pallas_call(
        lambda in_ref, out_ref: None,
        in_specs=[ANY],
        out_specs=ANY,
        out_shape=jax.ShapeDtypeStruct(part.shape, part.dtype),
        input_output_aliases={0: 0},
        cost_estimate=pl.CostEstimate(flops=COST, bytes_accessed=0, transcendentals=0),
        compiler_params=pltpu.CompilerParams(vmem_limit_bytes=MIB),
        name="settle",
    )(part)


def bring_kernel(*refs):
    arrived = refs[-1]
    count = len(refs) // 2
    copies = [pltpu.make_async_copy(refs[i], refs[count + i], arrived.at[i]) for i in range(count)]
    for copy in copies:
        copy.start()
    for copy in copies:
        copy.wait()


def bring(*there):
    return pl.pallas_call(
        bring_kernel,
        in_specs=[ANY] * len(there),
        out_specs=[VMEM] * len(there),
        out_shape=[pltpu.VMEM(x.shape, x.dtype) for x in there],
        scratch_shapes=[pltpu.SemaphoreType.DMA((len(there),))],
        cost_estimate=pl.CostEstimate(flops=0, bytes_accessed=sum(x.size * 4 for x in there), transcendentals=0),
        compiler_params=pltpu.CompilerParams(vmem_limit_bytes=MIB),
        name="bring",
    )(*there)


def exchange_kernel(count, d_own, d_other, b_own, b_other, out_ref, d, acc):
    core = lax.axis_index("c")
    for h, part in ((core, d_own), (1 - core, d_other)):
        for y in range(Y):
            for t in range(YROWS // STEP):
                rb = (y * YROWS + t * STEP) // BS
                here = slice(y * YROWS + t * STEP, y * YROWS + (t + 1) * STEP)
                for j in range(SENT // C):
                    col = lax.rem(rb + h * (SENT // C) + j, NB)
                    lanes = pl.ds(pl.multiple_of(col * BS, BS), BS)
                    d[here, lanes] = part[y, t * STEP : (t + 1) * STEP, j * BS : (j + 1) * BS]
    for rb in range(NB):
        for k in range(SENT, NB):
            cb = (rb + k) % NB
            rows, cols = slice(rb * BS, (rb + 1) * BS), slice(cb * BS, (cb + 1) * BS)
            d[rows, cols] = d[cols, rows].T
    unit = lax.broadcasted_iota(jnp.int32, (ROWS, 128), 1) // UNIT
    runs = [pl.ds(i * 2 * UNITS + core * UNITS, UNITS) for i in range(X // 2 * TILES)]
    for p in range(2 * count):
        b = b_own.at[p] if p < count else b_other.at[p - count]
        full = b[...].reshape(A, A)
        rows = jnp.concatenate([b[run].reshape(UNITS * G, A) for run in runs], 0)
        half = jnp.dot(rows, d[...], preferred_element_type=jnp.float32).astype(jnp.bfloat16)
        term = lax.dot_general(half, full, (((1,), (1,)), ((), ())), preferred_element_type=jnp.float32)
        acc[...] = term if p == 0 else acc[...] + term
    for yl in range(2):
        at = []
        for yp in range(YP):
            for t in range(ROWS // G):
                z, x = divmod((2 * yp + yl) * (YROWS // G) + 2 * t, X)
                run, group = divmod(place(z, x), 2 * UNITS)
                at.append((run * UNITS + group) * G)
        for i in range(X // 2 * TILES):
            lanes = slice(i * 128, (i + 1) * 128)
            tiles = [acc[r : r + G, lanes] for r in at]
            tiles = [jnp.concatenate(tiles[yp * (ROWS // G) : (yp + 1) * (ROWS // G)], 0) for yp in range(YP)]
            for j in range(UNITS):
                out = tiles[j]
                for yp in range(YP):
                    if yp != j:
                        out = jnp.where(unit == yp, pltpu.roll(tiles[yp], (yp - j) % UNITS * UNIT, 1), out)
                x, zl = i // TILES * 2 + j // 2, j % 2
                here = slice(i % TILES * ROWS, (i % TILES + 1) * ROWS)
                out_ref[(x * 2 + yl) * 2 + zl, here] = out.astype(jnp.bfloat16)


def exchange_rows(d_own, d_other, b_own, b_other):
    count = b_own.shape[0]
    return pl.pallas_call(
        functools.partial(exchange_kernel, count),
        in_specs=[VMEM, VMEM, VMEM, VMEM],
        out_specs=VMEM,
        out_shape=pltpu.VMEM((X * 4, TILES * ROWS, 128), jnp.bfloat16),
        scratch_shapes=[
            pltpu.VMEM((A, A), jnp.bfloat16),
            pltpu.VMEM((Y * ROWS, A), jnp.float32),
        ],
        compiler_params=pltpu.CompilerParams(vmem_limit_bytes=24 * MIB),
        name="exchange",
    )(vmem(d_own), vmem(d_other), vmem(b_own), vmem(b_other))


def pack_kernel(d_pattern, density, out_ref):
    y, core = lax.axis_index("yp") * 2 + lax.axis_index("yl"), lax.axis_index("c")
    for t in range(YROWS // STEP):
        rb = lax.div(y * YROWS + t * STEP, BS)
        for j in range(SENT // C):
            col = lax.rem(rb + core * (SENT // C) + j, NB)
            keep = jnp.maximum(d_pattern[rb, col], d_pattern[col, rb]) > 0
            block = density[t * STEP : (t + 1) * STEP, pl.ds(pl.multiple_of(col * BS, BS), BS)]
            block = jnp.where(keep, block, jnp.zeros_like(block))
            for to in range(Y):
                out_ref[to, t * STEP : (t + 1) * STEP, j * BS : (j + 1) * BS] = block


def pack_density(d_pattern, density):
    return pl.pallas_call(
        pack_kernel,
        in_specs=[SMEM, VMEM],
        out_specs=VMEM,
        out_shape=pltpu.VMEM((Y, YROWS, SENT // C * BS), jnp.bfloat16),
        compiler_params=pltpu.CompilerParams(vmem_limit_bytes=8 * MIB),
        name="pack",
    )(hbm(d_pattern), hbm(density))


def sum_near_kernel(in_ref, out_ref):
    total = in_ref[0].astype(jnp.float32)
    for i in range(1, X * 4):
        total = total + in_ref[i].astype(jnp.float32)
    for i in range(TILES):
        part = total[i * ROWS : (i + 1) * ROWS].T
        part = part.reshape(YP, 2 * C, K, ROWS)
        pad = jnp.zeros((YP, 2 * C, K // 2, 128 - 2 * ROWS), jnp.float32)
        out_ref[:, i * 2 * C : (i + 1) * 2 * C] = jnp.concatenate([part[:, :, : K // 2], part[:, :, K // 2 :], pad], 3)


def sum_near(parts):
    return pl.pallas_call(
        sum_near_kernel,
        in_specs=[VMEM],
        out_specs=VMEM,
        out_shape=pltpu.VMEM((YP, ZP * C, K // 2, 128), jnp.float32),
        compiler_params=pltpu.CompilerParams(vmem_limit_bytes=8 * MIB),
        name="sum_near",
    )(vmem(parts))


def sum_far_kernel(factor, in_ref, out_ref):
    halves = []
    for c in range(C):
        total = in_ref[c]
        for i in range(1, YP * ZP):
            total = total + in_ref[i * C + c]
        total = jnp.concatenate([total[:, :ROWS], total[:, ROWS : 2 * ROWS]], 0)
        halves.append(total * factor)
    out_ref[...] = jnp.concatenate([halves[g % C][:, g // C * G : (g // C + 1) * G] for g in range(YROWS // G)], 1)


def sum_far(parts, factor):
    return pl.pallas_call(
        functools.partial(sum_far_kernel, factor),
        in_specs=[VMEM],
        out_specs=VMEM,
        out_shape=jax.ShapeDtypeStruct((K, YROWS), jnp.float32),
        compiler_params=pltpu.CompilerParams(vmem_limit_bytes=4 * MIB),
        name="sum_far",
    )(vmem(parts))


def per_device(three_center, b_pattern, density, d_pattern):
    swap = [(0, 1), (1, 0)]
    mine = pack_density(d_pattern, density)
    mine, b_pattern = lax.optimization_barrier((mine, b_pattern))
    b_own = mask_and_order(three_center, b_pattern)
    b_other = lax.ppermute(b_own, "c", swap)
    d_own = settle(lax.all_to_all(mine, ("yp", "yl"), 0, 0, tiled=True))
    d_own, b_own, b_other = lax.optimization_barrier((d_own, b_own, b_other))
    d_other = lax.ppermute(d_own, "c", swap)
    parts = exchange_rows(d_own, d_other, *bring(b_own, b_other))
    parts = lax.all_to_all(parts, ("x", "yl", "zl"), 0, 0, tiled=True)
    parts = sum_near(parts).reshape(YP * ZP * C, K // 2, 128)
    parts = lax.all_to_all(parts, ("yp", "zp", "c"), 0, 0, tiled=True)
    total_ri = three_center.shape[0] * Z * X * C * Y
    return sum_far(parts, 1.0 / math.sqrt(total_ri * A)).T


def solution(mesh):
    every = ("zp", "zl", "x", "c", "yp", "yl")
    fine = Mesh(mesh.devices.reshape(ZP, 2, X, C, YP, 2), every)
    return jax.shard_map(
        per_device,
        mesh=fine,
        in_specs=(P(every, None, None), P(every, None, None), P(("yp", "yl"), None), P()),
        out_specs=P(("yp", "yl"), ("zp", "zl", "x", "c")),
        check_vma=False,
    )
```

```python
import functools
import math

import jax
import jax.numpy as jnp
from jax import lax
from jax.experimental import pallas as pl
from jax.experimental.pallas import tpu as pltpu
from jax.sharding import Mesh, PartitionSpec as P

Z, X, C, Y = 12, 4, 2, 8
A, BS, NB = 768, 128, 6
K = 8
G = 16
GROUPS = A // G
ROWS = A // (Y * C)
YROWS = A // Y
STEP = 32
SENT = 4
PACK = ROWS * Z * G // 128
MAIN = 128 // G
COST = 10**11
MIB = 1024 * 1024
VMEM = pl.BlockSpec(memory_space=pltpu.VMEM)
SMEM = pl.BlockSpec(memory_space=pltpu.SMEM)
ANY = pl.BlockSpec(memory_space=pl.ANY)


def hbm(x):
    return pltpu.with_memory_space_constraint(x, pltpu.HBM)


def vmem(x):
    return pltpu.with_memory_space_constraint(x, pltpu.VMEM)


def place(z, x):
    return x * Z + z


def mask_kernel(pattern, b_ref, out_ref):
    p = pl.program_id(0)
    for rb in range(NB):
        for cb in range(NB):
            keep = pattern[rb, p, cb] > 0
            lanes = slice(cb * BS, (cb + 1) * BS)
            for g in range(rb * 8, rb * 8 + 8):
                block = b_ref[0, g, :, lanes]
                out_ref[0, place(g // X, g % X), :, lanes] = jnp.where(keep, block, jnp.zeros_like(block))


def mask_and_order(three_center, b_pattern):
    count = three_center.shape[0]
    spec = pl.BlockSpec((1, GROUPS, G, A), lambda p: (p, 0, 0, 0))
    return pl.pallas_call(
        mask_kernel,
        grid=(count,),
        in_specs=[SMEM, spec],
        out_specs=spec,
        out_shape=pltpu.VMEM((count, GROUPS, G, A), jnp.bfloat16),
        cost_estimate=pl.CostEstimate(flops=COST, bytes_accessed=0, transcendentals=0),
        compiler_params=pltpu.CompilerParams(vmem_limit_bytes=16 * MIB),
        name="mask",
    )(hbm(b_pattern.transpose(1, 0, 2)), hbm(three_center.reshape(count, GROUPS, G, A)))


def settle(part):
    return pl.pallas_call(
        lambda in_ref, out_ref: None,
        in_specs=[ANY],
        out_specs=ANY,
        out_shape=jax.ShapeDtypeStruct(part.shape, part.dtype),
        input_output_aliases={0: 0},
        cost_estimate=pl.CostEstimate(flops=COST, bytes_accessed=0, transcendentals=0),
        compiler_params=pltpu.CompilerParams(vmem_limit_bytes=MIB),
        name="settle",
    )(part)


def bring_kernel(*refs):
    arrived = refs[-1]
    count = len(refs) // 2
    copies = [pltpu.make_async_copy(refs[i], refs[count + i], arrived.at[i]) for i in range(count)]
    for copy in copies:
        copy.start()
    for copy in copies:
        copy.wait()


def bring(*there):
    return pl.pallas_call(
        bring_kernel,
        in_specs=[ANY] * len(there),
        out_specs=[VMEM] * len(there),
        out_shape=[pltpu.VMEM(x.shape, x.dtype) for x in there],
        scratch_shapes=[pltpu.SemaphoreType.DMA((len(there),))],
        cost_estimate=pl.CostEstimate(flops=0, bytes_accessed=sum(x.size * 4 for x in there), transcendentals=0),
        compiler_params=pltpu.CompilerParams(vmem_limit_bytes=MIB),
        name="bring",
    )(*there)


def exchange_kernel(count, d_own, d_other, b_own, b_other, out_ref, d, acc):
    core = lax.axis_index("c")
    for h, part in ((core, d_own), (1 - core, d_other)):
        for y in range(Y):
            for t in range(YROWS // STEP):
                rb = (y * YROWS + t * STEP) // BS
                here = slice(y * YROWS + t * STEP, y * YROWS + (t + 1) * STEP)
                for j in range(SENT // C):
                    col = lax.rem(rb + h * (SENT // C) + j, NB)
                    lanes = pl.ds(pl.multiple_of(col * BS, BS), BS)
                    d[here, lanes] = part[y, t * STEP : (t + 1) * STEP, j * BS : (j + 1) * BS]
    for rb in range(NB):
        for k in range(SENT, NB):
            cb = (rb + k) % NB
            rows, cols = slice(rb * BS, (rb + 1) * BS), slice(cb * BS, (cb + 1) * BS)
            d[rows, cols] = d[cols, rows].T
    lane = lax.broadcasted_iota(jnp.int32, (ROWS // 2, 128), 1)
    top, bottom = slice(0, ROWS // 2), slice(ROWS // 2, ROWS)
    half_rows, halves = Z * G, X // 2
    for p in range(2 * count):
        b = b_own.at[p] if p < count else b_other.at[p - count]
        full = b[...].reshape(A, A)
        rows = [b[pl.ds((2 * q + core) * Z, Z)].reshape(half_rows, A) for q in range(halves)]
        half = jnp.dot(jnp.concatenate(rows, 0), d[...], preferred_element_type=jnp.float32).astype(jnp.bfloat16)
        term = lax.dot_general(half, full, (((1,), (1,)), ((), ())), preferred_element_type=jnp.float32)
        acc[...] = term if p == 0 else acc[...] + term
    for y in range(Y):
        at = []
        for t in range(ROWS // G):
            z, x = divmod(y * (YROWS // G) + 2 * t, X)
            at.append((x // 2) * half_rows + z * G)
        for q in range(halves):
            left, middle, right = [
                jnp.concatenate([acc[r : r + G, (3 * q + i) * 128 : (3 * q + i + 1) * 128] for r in at], 0)
                for i in range(3)
            ]
            turned = pltpu.roll(middle, 64, 1)
            even = jnp.where(lane < 64, middle[top], turned[bottom])
            odd = jnp.where(lane < 64, turned[top], middle[bottom])
            out_ref[y * X + 2 * q] = jnp.concatenate([left, even], 0).astype(jnp.bfloat16)
            out_ref[y * X + 2 * q + 1] = jnp.concatenate([right, odd], 0).astype(jnp.bfloat16)


def exchange_rows(d_own, d_other, b_own, b_other):
    count = b_own.shape[0]
    return pl.pallas_call(
        functools.partial(exchange_kernel, count),
        in_specs=[VMEM, VMEM, VMEM, VMEM],
        out_specs=VMEM,
        out_shape=pltpu.VMEM((X * Y, PACK, 128), jnp.bfloat16),
        scratch_shapes=[
            pltpu.VMEM((A, A), jnp.bfloat16),
            pltpu.VMEM((Y * ROWS, A), jnp.float32),
        ],
        compiler_params=pltpu.CompilerParams(vmem_limit_bytes=24 * MIB),
        name="exchange",
    )(vmem(d_own), vmem(d_other), vmem(b_own), vmem(b_other))


def pack_kernel(d_pattern, density, out_ref):
    y, core = lax.axis_index("y"), lax.axis_index("c")
    for t in range(YROWS // STEP):
        rb = lax.div(y * YROWS + t * STEP, BS)
        for j in range(SENT // C):
            col = lax.rem(rb + core * (SENT // C) + j, NB)
            keep = jnp.maximum(d_pattern[rb, col], d_pattern[col, rb]) > 0
            block = density[t * STEP : (t + 1) * STEP, pl.ds(pl.multiple_of(col * BS, BS), BS)]
            block = jnp.where(keep, block, jnp.zeros_like(block))
            for to in range(Y):
                out_ref[to, t * STEP : (t + 1) * STEP, j * BS : (j + 1) * BS] = block


def pack_density(d_pattern, density):
    return pl.pallas_call(
        pack_kernel,
        in_specs=[SMEM, VMEM],
        out_specs=VMEM,
        out_shape=pltpu.VMEM((Y, YROWS, SENT // C * BS), jnp.bfloat16),
        compiler_params=pltpu.CompilerParams(vmem_limit_bytes=8 * MIB),
        name="pack",
    )(hbm(d_pattern), hbm(density))


def sum_xy_kernel(in_ref, out_ref):
    total = in_ref[0].astype(jnp.float32)
    for i in range(1, X * Y):
        total = total + in_ref[i].astype(jnp.float32)
    first, rest = total[:ROWS].T, total[ROWS:].T
    rest = jnp.concatenate([rest[:64], rest[64:]], 1)
    odd = lax.rem(lax.axis_index("x"), 2)
    for part, at in ((first, odd * (Z - MAIN) * C), (rest, (1 - odd) * MAIN * C)):
        count = part.shape[0] // K
        part = part.reshape(count, K, ROWS)
        pad = jnp.zeros((count, K // 2, 128 - 2 * ROWS), jnp.float32)
        out_ref[pl.ds(at, count)] = jnp.concatenate([part[:, : K // 2], part[:, K // 2 :], pad], 2)


def sum_xy(parts):
    return pl.pallas_call(
        sum_xy_kernel,
        in_specs=[VMEM],
        out_specs=VMEM,
        out_shape=pltpu.VMEM((Z * C, K // 2, 128), jnp.float32),
        compiler_params=pltpu.CompilerParams(vmem_limit_bytes=8 * MIB),
        name="sum_xy",
    )(vmem(parts))


def sum_z_kernel(factor, in_ref, out_ref):
    halves = []
    for c in range(C):
        total = in_ref[c]
        for z in range(1, Z):
            total = total + in_ref[z * C + c]
        total = jnp.concatenate([total[:, :ROWS], total[:, ROWS : 2 * ROWS]], 0)
        halves.append(total * factor)
    out_ref[...] = jnp.concatenate([halves[g % C][:, g // C * G : (g // C + 1) * G] for g in range(YROWS // G)], 1)


def sum_z(parts, factor):
    return pl.pallas_call(
        functools.partial(sum_z_kernel, factor),
        in_specs=[VMEM],
        out_specs=VMEM,
        out_shape=jax.ShapeDtypeStruct((K, YROWS), jnp.float32),
        compiler_params=pltpu.CompilerParams(vmem_limit_bytes=4 * MIB),
        name="sum_z",
    )(vmem(parts))


def per_device(three_center, b_pattern, density, d_pattern):
    swap = [(0, 1), (1, 0)]
    mine = pack_density(d_pattern, density)
    mine, b_pattern = lax.optimization_barrier((mine, b_pattern))
    b_own = mask_and_order(three_center, b_pattern)
    b_other = lax.ppermute(b_own, "c", swap)
    d_own = settle(lax.all_to_all(mine, "y", 0, 0, tiled=True))
    d_own, b_own, b_other = lax.optimization_barrier((d_own, b_own, b_other))
    d_other = lax.ppermute(d_own, "c", swap)
    parts = exchange_rows(d_own, d_other, *bring(b_own, b_other))
    parts = lax.all_to_all(parts, ("y", "x"), 0, 0, tiled=True)
    parts = lax.all_to_all(sum_xy(parts), ("z", "c"), 0, 0, tiled=True)
    total_ri = three_center.shape[0] * Z * X * C * Y
    return sum_z(parts, 1.0 / math.sqrt(total_ri * A)).T


def solution(mesh):
    fine = Mesh(mesh.devices.reshape(Z, X, C, Y), ("z", "x", "c", "y"))
    every = ("z", "x", "c", "y")
    return jax.shard_map(
        per_device,
        mesh=fine,
        in_specs=(P(every, None, None), P(every, None, None), P("y", None), P()),
        out_specs=P("y", ("z", "x", "c")),
        check_vma=False,
    )
```

```python
import functools
import math

import jax
import jax.numpy as jnp
from jax import lax
from jax.experimental import pallas as pl
from jax.experimental.pallas import tpu as pltpu
from jax.sharding import Mesh, PartitionSpec as P

Z, X, C, Y = 12, 4, 2, 8
A, BS, NB = 768, 128, 6
K = 8
G = 16
GROUPS = A // G
ROWS = A // (Y * C)
YROWS = A // Y
STEP = 32
SENT = 4
PACK = ROWS * Z * G // 128
MAIN = 128 // G
COST = 10**11
MIB = 1024 * 1024
VMEM = pl.BlockSpec(memory_space=pltpu.VMEM)
SMEM = pl.BlockSpec(memory_space=pltpu.SMEM)
ANY = pl.BlockSpec(memory_space=pl.ANY)


def hbm(x):
    return pltpu.with_memory_space_constraint(x, pltpu.HBM)


def vmem(x):
    return pltpu.with_memory_space_constraint(x, pltpu.VMEM)


def place(z, x):
    return x * Z + z


def mask_kernel(pattern, b_ref, out_ref):
    p = pl.program_id(0)
    for rb in range(NB):
        for cb in range(NB):
            keep = pattern[rb, p, cb] > 0
            lanes = slice(cb * BS, (cb + 1) * BS)
            for g in range(rb * 8, rb * 8 + 8):
                block = b_ref[0, g, :, lanes]
                out_ref[0, place(g // X, g % X), :, lanes] = jnp.where(keep, block, jnp.zeros_like(block))


def mask_and_order(three_center, b_pattern):
    count = three_center.shape[0]
    spec = pl.BlockSpec((1, GROUPS, G, A), lambda p: (p, 0, 0, 0))
    return pl.pallas_call(
        mask_kernel,
        grid=(count,),
        in_specs=[SMEM, spec],
        out_specs=spec,
        out_shape=pltpu.VMEM((count, GROUPS, G, A), jnp.bfloat16),
        cost_estimate=pl.CostEstimate(flops=COST, bytes_accessed=0, transcendentals=0),
        compiler_params=pltpu.CompilerParams(vmem_limit_bytes=16 * MIB),
        name="mask",
    )(hbm(b_pattern.transpose(1, 0, 2)), hbm(three_center.reshape(count, GROUPS, G, A)))


def settle(part):
    return pl.pallas_call(
        lambda in_ref, out_ref: None,
        in_specs=[ANY],
        out_specs=ANY,
        out_shape=jax.ShapeDtypeStruct(part.shape, part.dtype),
        input_output_aliases={0: 0},
        cost_estimate=pl.CostEstimate(flops=COST, bytes_accessed=0, transcendentals=0),
        compiler_params=pltpu.CompilerParams(vmem_limit_bytes=MIB),
        name="settle",
    )(part)


def bring_kernel(*refs):
    arrived = refs[-1]
    count = len(refs) // 2
    copies = [pltpu.make_async_copy(refs[i], refs[count + i], arrived.at[i]) for i in range(count)]
    for copy in copies:
        copy.start()
    for copy in copies:
        copy.wait()


def bring(*there):
    return pl.pallas_call(
        bring_kernel,
        in_specs=[ANY] * len(there),
        out_specs=[VMEM] * len(there),
        out_shape=[pltpu.VMEM(x.shape, x.dtype) for x in there],
        scratch_shapes=[pltpu.SemaphoreType.DMA((len(there),))],
        cost_estimate=pl.CostEstimate(flops=0, bytes_accessed=sum(x.size * 4 for x in there), transcendentals=0),
        compiler_params=pltpu.CompilerParams(vmem_limit_bytes=MIB),
        name="bring",
    )(*there)


def exchange_kernel(count, d_own, d_other, b_own, b_other, out_ref, d, acc):
    core = lax.axis_index("c")
    for h, part in ((core, d_own), (1 - core, d_other)):
        for y in range(Y):
            for t in range(YROWS // STEP):
                rb = (y * YROWS + t * STEP) // BS
                here = slice(y * YROWS + t * STEP, y * YROWS + (t + 1) * STEP)
                for j in range(SENT // C):
                    col = lax.rem(rb + h * (SENT // C) + j, NB)
                    lanes = pl.ds(pl.multiple_of(col * BS, BS), BS)
                    d[here, lanes] = part[y, t * STEP : (t + 1) * STEP, j * BS : (j + 1) * BS]
    for rb in range(NB):
        for k in range(SENT, NB):
            cb = (rb + k) % NB
            rows, cols = slice(rb * BS, (rb + 1) * BS), slice(cb * BS, (cb + 1) * BS)
            d[rows, cols] = d[cols, rows].T
    lane = lax.broadcasted_iota(jnp.int32, (ROWS // 2, 128), 1)
    top, bottom = slice(0, ROWS // 2), slice(ROWS // 2, ROWS)
    half_rows, halves = Z * G, X // 2
    for p in range(2 * count):
        b = b_own.at[p] if p < count else b_other.at[p - count]
        full = b[...].reshape(A, A)
        rows = [b[pl.ds((2 * q + core) * Z, Z)].reshape(half_rows, A) for q in range(halves)]
        half = jnp.dot(jnp.concatenate(rows, 0), d[...], preferred_element_type=jnp.float32).astype(jnp.bfloat16)
        term = lax.dot_general(half, full, (((1,), (1,)), ((), ())), preferred_element_type=jnp.float32)
        acc[...] = term if p == 0 else acc[...] + term
    for y in range(Y):
        at = []
        for t in range(ROWS // G):
            z, x = divmod(y * (YROWS // G) + 2 * t, X)
            at.append((x // 2) * half_rows + z * G)
        for q in range(halves):
            left, middle, right = [
                jnp.concatenate([acc[r : r + G, (3 * q + i) * 128 : (3 * q + i + 1) * 128] for r in at], 0)
                for i in range(3)
            ]
            turned = pltpu.roll(middle, 64, 1)
            even = jnp.where(lane < 64, middle[top], turned[bottom])
            odd = jnp.where(lane < 64, turned[top], middle[bottom])
            out_ref[(2 * q) * Y + y] = jnp.concatenate([left, even], 0).astype(jnp.bfloat16)
            out_ref[(2 * q + 1) * Y + y] = jnp.concatenate([right, odd], 0).astype(jnp.bfloat16)


def exchange_rows(d_own, d_other, b_own, b_other):
    count = b_own.shape[0]
    return pl.pallas_call(
        functools.partial(exchange_kernel, count),
        in_specs=[VMEM, VMEM, VMEM, VMEM],
        out_specs=VMEM,
        out_shape=pltpu.VMEM((X * Y, PACK, 128), jnp.bfloat16),
        scratch_shapes=[
            pltpu.VMEM((A, A), jnp.bfloat16),
            pltpu.VMEM((Y * ROWS, A), jnp.float32),
        ],
        compiler_params=pltpu.CompilerParams(vmem_limit_bytes=24 * MIB),
        name="exchange",
    )(vmem(d_own), vmem(d_other), vmem(b_own), vmem(b_other))


def pack_kernel(d_pattern, density, out_ref):
    y, core = lax.axis_index("y"), lax.axis_index("c")
    for t in range(YROWS // STEP):
        rb = lax.div(y * YROWS + t * STEP, BS)
        for j in range(SENT // C):
            col = lax.rem(rb + core * (SENT // C) + j, NB)
            keep = jnp.maximum(d_pattern[rb, col], d_pattern[col, rb]) > 0
            block = density[t * STEP : (t + 1) * STEP, pl.ds(pl.multiple_of(col * BS, BS), BS)]
            block = jnp.where(keep, block, jnp.zeros_like(block))
            for to in range(Y):
                out_ref[to, t * STEP : (t + 1) * STEP, j * BS : (j + 1) * BS] = block


def pack_density(d_pattern, density):
    return pl.pallas_call(
        pack_kernel,
        in_specs=[SMEM, VMEM],
        out_specs=VMEM,
        out_shape=pltpu.VMEM((Y, YROWS, SENT // C * BS), jnp.bfloat16),
        compiler_params=pltpu.CompilerParams(vmem_limit_bytes=8 * MIB),
        name="pack",
    )(hbm(d_pattern), hbm(density))


def sum_xy_kernel(in_ref, out_ref):
    total = in_ref[0].astype(jnp.float32)
    for i in range(1, X * Y):
        total = total + in_ref[i].astype(jnp.float32)
    first, rest = total[:ROWS].T, total[ROWS:].T
    rest = jnp.concatenate([rest[:64], rest[64:]], 1)
    odd = lax.rem(lax.axis_index("x"), 2)
    for part, at in ((first, odd * (Z - MAIN) * C), (rest, (1 - odd) * MAIN * C)):
        count = part.shape[0] // K
        part = part.reshape(count, K, ROWS)
        pad = jnp.zeros((count, K // 2, 128 - 2 * ROWS), jnp.float32)
        packed = jnp.concatenate([part[:, : K // 2], part[:, K // 2 :], pad], 2)
        out_ref[pl.ds(at, count)] = packed.astype(jnp.bfloat16)


def sum_xy(parts):
    return pl.pallas_call(
        sum_xy_kernel,
        in_specs=[VMEM],
        out_specs=VMEM,
        out_shape=pltpu.VMEM((Z * C, K // 2, 128), jnp.bfloat16),
        compiler_params=pltpu.CompilerParams(vmem_limit_bytes=8 * MIB),
        name="sum_xy",
    )(vmem(parts))


def sum_z_kernel(factor, in_ref, out_ref):
    halves = []
    for c in range(C):
        total = in_ref[c].astype(jnp.float32)
        for z in range(1, Z):
            total = total + in_ref[z * C + c].astype(jnp.float32)
        total = jnp.concatenate([total[:, :ROWS], total[:, ROWS : 2 * ROWS]], 0)
        halves.append(total * factor)
    out_ref[...] = jnp.concatenate([halves[g % C][:, g // C * G : (g // C + 1) * G] for g in range(YROWS // G)], 1)


def sum_z(parts, factor):
    return pl.pallas_call(
        functools.partial(sum_z_kernel, factor),
        in_specs=[VMEM],
        out_specs=VMEM,
        out_shape=jax.ShapeDtypeStruct((K, YROWS), jnp.float32),
        compiler_params=pltpu.CompilerParams(vmem_limit_bytes=4 * MIB),
        name="sum_z",
    )(vmem(parts))


def per_device(three_center, b_pattern, density, d_pattern):
    swap = [(0, 1), (1, 0)]
    mine = pack_density(d_pattern, density)
    mine, b_pattern = lax.optimization_barrier((mine, b_pattern))
    b_own = mask_and_order(three_center, b_pattern)
    b_other = lax.ppermute(b_own, "c", swap)
    d_own = settle(lax.all_to_all(mine, "y", 0, 0, tiled=True))
    d_own, b_own, b_other = lax.optimization_barrier((d_own, b_own, b_other))
    d_other = lax.ppermute(d_own, "c", swap)
    parts = exchange_rows(d_own, d_other, *bring(b_own, b_other))
    parts = lax.all_to_all(parts, ("x", "y"), 0, 0, tiled=True)
    parts = lax.all_to_all(sum_xy(parts), ("z", "c"), 0, 0, tiled=True)
    total_ri = three_center.shape[0] * Z * X * C * Y
    return sum_z(parts, 1.0 / math.sqrt(total_ri * A)).T


def solution(mesh):
    fine = Mesh(mesh.devices.reshape(Z, X, C, Y), ("z", "x", "c", "y"))
    every = ("z", "x", "c", "y")
    return jax.shard_map(
        per_device,
        mesh=fine,
        in_specs=(P(every, None, None), P(every, None, None), P("y", None), P()),
        out_specs=P("y", ("z", "x", "c")),
        check_vma=False,
    )
```

```python
import functools
import math

import jax
import jax.numpy as jnp
from jax import lax
from jax.experimental import pallas as pl
from jax.experimental.pallas import tpu as pltpu
from jax.sharding import Mesh, PartitionSpec as P

Z, X, C, Y = 12, 4, 2, 8
A, BS, NB = 768, 128, 6
K = 8
G = 16
GROUPS = A // G
ROWS = A // (Y * C)
YROWS = A // Y
STEP = 32
SENT = 4
PACK = ROWS * Z * G // 128
MAIN = 128 // G
COST = 10**11
MIB = 1024 * 1024
VMEM = pl.BlockSpec(memory_space=pltpu.VMEM)
SMEM = pl.BlockSpec(memory_space=pltpu.SMEM)
ANY = pl.BlockSpec(memory_space=pl.ANY)


def hbm(x):
    return pltpu.with_memory_space_constraint(x, pltpu.HBM)


def vmem(x):
    return pltpu.with_memory_space_constraint(x, pltpu.VMEM)


def place(z, x):
    return x * Z + z


def mask_kernel(pattern, b_ref, out_ref):
    p = pl.program_id(0)
    for rb in range(NB):
        for cb in range(NB):
            keep = pattern[rb, p, cb] > 0
            lanes = slice(cb * BS, (cb + 1) * BS)
            for g in range(rb * 8, rb * 8 + 8):
                block = b_ref[0, g, :, lanes]
                out_ref[0, place(g // X, g % X), :, lanes] = jnp.where(keep, block, jnp.zeros_like(block))


def mask_and_order(three_center, b_pattern):
    count = three_center.shape[0]
    spec = pl.BlockSpec((1, GROUPS, G, A), lambda p: (p, 0, 0, 0))
    return pl.pallas_call(
        mask_kernel,
        grid=(count,),
        in_specs=[SMEM, spec],
        out_specs=spec,
        out_shape=pltpu.VMEM((count, GROUPS, G, A), jnp.bfloat16),
        cost_estimate=pl.CostEstimate(flops=COST, bytes_accessed=0, transcendentals=0),
        compiler_params=pltpu.CompilerParams(vmem_limit_bytes=16 * MIB),
        name="mask",
    )(hbm(b_pattern.transpose(1, 0, 2)), hbm(three_center.reshape(count, GROUPS, G, A)))


def settle(part):
    return pl.pallas_call(
        lambda in_ref, out_ref: None,
        in_specs=[ANY],
        out_specs=ANY,
        out_shape=jax.ShapeDtypeStruct(part.shape, part.dtype),
        input_output_aliases={0: 0},
        cost_estimate=pl.CostEstimate(flops=COST, bytes_accessed=0, transcendentals=0),
        compiler_params=pltpu.CompilerParams(vmem_limit_bytes=MIB),
        name="settle",
    )(part)


def lay(part, h, d):
    for y in range(Y):
        for t in range(YROWS // STEP):
            rb = (y * YROWS + t * STEP) // BS
            here = slice(y * YROWS + t * STEP, y * YROWS + (t + 1) * STEP)
            for j in range(SENT // C):
                col = lax.rem(rb + h * (SENT // C) + j, NB)
                lanes = pl.ds(pl.multiple_of(col * BS, BS), BS)
                d[here, lanes] = part[y, t * STEP : (t + 1) * STEP, j * BS : (j + 1) * BS]
    for rb in range(NB):
        to = pl.ds(pl.multiple_of(lax.rem(rb + 1 + h, NB) * BS, BS), BS)
        rows = slice(rb * BS, (rb + 1) * BS)
        d[to, rows] = d[rows, to].T


def bring_kernel(part, *refs):
    *there, d, arrived = refs
    count = len(there) // 2
    copies = [pltpu.make_async_copy(there[i], there[count + i], arrived.at[i]) for i in range(count)]
    for copy in copies:
        copy.start()
    lay(part, lax.axis_index("c"), d)
    for copy in copies:
        copy.wait()


def bring(part, *there):
    return pl.pallas_call(
        bring_kernel,
        in_specs=[VMEM] + [ANY] * len(there),
        out_specs=[VMEM] * (len(there) + 1),
        out_shape=[pltpu.VMEM(x.shape, x.dtype) for x in there] + [pltpu.VMEM((A, A), part.dtype)],
        scratch_shapes=[pltpu.SemaphoreType.DMA((len(there),))],
        cost_estimate=pl.CostEstimate(flops=0, bytes_accessed=sum(x.size * 4 for x in there), transcendentals=0),
        compiler_params=pltpu.CompilerParams(vmem_limit_bytes=MIB),
        name="bring",
    )(vmem(part), *there)


def exchange_kernel(count, d_other, b_own, b_other, d_half, out_ref, d, acc):
    del d_half
    core = lax.axis_index("c")
    lay(d_other, 1 - core, d)
    lane = lax.broadcasted_iota(jnp.int32, (ROWS // 2, 128), 1)
    top, bottom = slice(0, ROWS // 2), slice(ROWS // 2, ROWS)
    half_rows, halves = Z * G, X // 2
    for p in range(2 * count):
        b = b_own.at[p] if p < count else b_other.at[p - count]
        full = b[...].reshape(A, A)
        rows = [b[pl.ds((2 * q + core) * Z, Z)].reshape(half_rows, A) for q in range(halves)]
        half = jnp.dot(jnp.concatenate(rows, 0), d[...], preferred_element_type=jnp.float32).astype(jnp.bfloat16)
        term = lax.dot_general(half, full, (((1,), (1,)), ((), ())), preferred_element_type=jnp.float32)
        acc[...] = term if p == 0 else acc[...] + term
    for y in range(Y):
        at = []
        for t in range(ROWS // G):
            z, x = divmod(y * (YROWS // G) + 2 * t, X)
            at.append((x // 2) * half_rows + z * G)
        for q in range(halves):
            left, middle, right = [
                jnp.concatenate([acc[r : r + G, (3 * q + i) * 128 : (3 * q + i + 1) * 128] for r in at], 0)
                for i in range(3)
            ]
            turned = pltpu.roll(middle, 64, 1)
            even = jnp.where(lane < 64, middle[top], turned[bottom])
            odd = jnp.where(lane < 64, turned[top], middle[bottom])
            out_ref[y * X + 2 * q] = jnp.concatenate([left, even], 0).astype(jnp.bfloat16)
            out_ref[y * X + 2 * q + 1] = jnp.concatenate([right, odd], 0).astype(jnp.bfloat16)


def exchange_rows(d_other, b_own, b_other, d):
    count = b_own.shape[0]
    return pl.pallas_call(
        functools.partial(exchange_kernel, count),
        in_specs=[VMEM, VMEM, VMEM, VMEM],
        out_specs=[VMEM, VMEM],
        out_shape=[pltpu.VMEM((X * Y, PACK, 128), jnp.bfloat16), pltpu.VMEM((A, A), jnp.bfloat16)],
        input_output_aliases={3: 1},
        scratch_shapes=[pltpu.VMEM((Y * ROWS, A), jnp.float32)],
        compiler_params=pltpu.CompilerParams(vmem_limit_bytes=24 * MIB),
        name="exchange",
    )(vmem(d_other), vmem(b_own), vmem(b_other), vmem(d))[0]


def pack_kernel(d_pattern, density, out_ref):
    y, core = lax.axis_index("y"), lax.axis_index("c")
    for t in range(YROWS // STEP):
        rb = lax.div(y * YROWS + t * STEP, BS)
        for j in range(SENT // C):
            col = lax.rem(rb + core * (SENT // C) + j, NB)
            keep = jnp.maximum(d_pattern[rb, col], d_pattern[col, rb]) > 0
            block = density[t * STEP : (t + 1) * STEP, pl.ds(pl.multiple_of(col * BS, BS), BS)]
            block = jnp.where(keep, block, jnp.zeros_like(block))
            for to in range(Y):
                out_ref[to, t * STEP : (t + 1) * STEP, j * BS : (j + 1) * BS] = block


def pack_density(d_pattern, density):
    return pl.pallas_call(
        pack_kernel,
        in_specs=[SMEM, VMEM],
        out_specs=VMEM,
        out_shape=pltpu.VMEM((Y, YROWS, SENT // C * BS), jnp.bfloat16),
        compiler_params=pltpu.CompilerParams(vmem_limit_bytes=8 * MIB),
        name="pack",
    )(hbm(d_pattern), hbm(density))


def sum_xy_kernel(in_ref, out_ref):
    total = in_ref[0].astype(jnp.float32)
    for i in range(1, X * Y):
        total = total + in_ref[i].astype(jnp.float32)
    first, rest = total[:ROWS].T, total[ROWS:].T
    rest = jnp.concatenate([rest[:64], rest[64:]], 1)
    odd = lax.rem(lax.axis_index("x"), 2)
    for part, at in ((first, odd * (Z - MAIN) * C), (rest, (1 - odd) * MAIN * C)):
        count = part.shape[0] // K
        part = part.reshape(count, K, ROWS)
        pad = jnp.zeros((count, K // 2, 128 - 2 * ROWS), jnp.float32)
        out_ref[pl.ds(at, count)] = jnp.concatenate([part[:, : K // 2], part[:, K // 2 :], pad], 2)


def sum_xy(parts):
    return pl.pallas_call(
        sum_xy_kernel,
        in_specs=[VMEM],
        out_specs=VMEM,
        out_shape=pltpu.VMEM((Z * C, K // 2, 128), jnp.float32),
        compiler_params=pltpu.CompilerParams(vmem_limit_bytes=8 * MIB),
        name="sum_xy",
    )(vmem(parts))


def sum_z_kernel(factor, in_ref, out_ref):
    halves = []
    for c in range(C):
        total = in_ref[c]
        for z in range(1, Z):
            total = total + in_ref[z * C + c]
        total = jnp.concatenate([total[:, :ROWS], total[:, ROWS : 2 * ROWS]], 0)
        halves.append(total * factor)
    out_ref[...] = jnp.concatenate([halves[g % C][:, g // C * G : (g // C + 1) * G] for g in range(YROWS // G)], 1)


def sum_z(parts, factor):
    return pl.pallas_call(
        functools.partial(sum_z_kernel, factor),
        in_specs=[VMEM],
        out_specs=VMEM,
        out_shape=jax.ShapeDtypeStruct((K, YROWS), jnp.float32),
        compiler_params=pltpu.CompilerParams(vmem_limit_bytes=4 * MIB),
        name="sum_z",
    )(vmem(parts))


def per_device(three_center, b_pattern, density, d_pattern):
    swap = [(0, 1), (1, 0)]
    mine = pack_density(d_pattern, density)
    mine, b_pattern = lax.optimization_barrier((mine, b_pattern))
    b_own = mask_and_order(three_center, b_pattern)
    b_other = lax.ppermute(b_own, "c", swap)
    d_own = settle(lax.all_to_all(mine, "y", 0, 0, tiled=True))
    d_own, b_own, b_other = lax.optimization_barrier((d_own, b_own, b_other))
    d_other = lax.ppermute(d_own, "c", swap)
    parts = exchange_rows(d_other, *bring(d_own, b_own, b_other))
    parts = lax.all_to_all(parts, ("y", "x"), 0, 0, tiled=True)
    parts = lax.all_to_all(sum_xy(parts), ("z", "c"), 0, 0, tiled=True)
    total_ri = three_center.shape[0] * Z * X * C * Y
    return sum_z(parts, 1.0 / math.sqrt(total_ri * A)).T


def solution(mesh):
    fine = Mesh(mesh.devices.reshape(Z, X, C, Y), ("z", "x", "c", "y"))
    every = ("z", "x", "c", "y")
    return jax.shard_map(
        per_device,
        mesh=fine,
        in_specs=(P(every, None, None), P(every, None, None), P("y", None), P()),
        out_specs=P("y", ("z", "x", "c")),
        check_vma=False,
    )
```
